32 devices in a mesh: groups: 2 (over y), lat: 4 (over z), layer: 2 (over x), tok: 2 (over core).
Axes of the slice: x: 2, y: 2, z: 4, core: 2. Of those that a mesh axis runs over, the one named last changes fastest.
Arguments:
- tokens: bfloat16 [1024, 2, 2304], P(('groups', 'lat'), 'layer'), parts along dimension 0, may hold values from -6 to 6
- w_enc: bfloat16 [2, 2304, 8192], P('layer', None, ('lat', 'tok')), may hold values from -0.09375 to 0.09375
- b_enc: float32 [8192], P(('lat', 'tok')), may hold values from -3 to 3
- w_dec: bfloat16 [2, 8192, 2304], P('layer', ('lat', 'tok')), may hold values from -0.25 to 0.25
- b_dec: float32 [2, 2304], P('layer'), may hold values from -3 to 3
- block_ids: int32 [8, 16], P('groups'), parts along dimension 0, may hold values from 0 to 127, as said below
- counts: int32 [8], P('groups'), parts along dimension 0, may hold values from 8 to 16, as said below
Outputs:
- residual: bfloat16 [1024, 2, 2304], P(('groups', 'lat'), 'layer'), parts along dimension 0
- scale_grad: float32 [16384], P(('groups', 'lat', 'tok')), parts along dimension 0
The draws below stay inside these ranges and needn't reach their ends.
There are 2 independent parts, one for each index of `groups`. The reference program is written for one: setup_inputs(seed, part) draws one part's arguments, and reference() takes and returns one part's arrays. A program takes and returns all parts, laid end to end along the dimension named above; an argument that names none is the same for every part. Nothing has to cross between parts.
Inputs may be any that keep to these rules, and one draw needn't show every extreme that they name: `block_ids`: within one token block the 16 slots name distinct latent blocks; of the blocks k * 16 to (k + 1) * 16 - 1 of one latent shard k, at most 3 are named by live slots of one token block, and in every token block some shard has exactly 3. `counts`: some token block has all 16 slots live.
All inputs are finite; a program needn't handle non-finite values.
Results may differ from the reference program's by a relative error of at most 0.013.
Values may be sent and summed in bfloat16 or wider, within the bound.
No kernel may reach another device: no remote copies, remote signals or barrier semaphores. Data moves between devices by JAX's collectives and lax.ppermute only.
A program may use at most 64 MiB of HBM per device.

```python
import jax
import jax.numpy as jnp
from jax import lax

D = 2304
LAT_DEV = 1024
LATBLK = 64
TBLK = 128
CAP = 3
NL = 2
TOKENS = 512
LAT = 8192
NBLK = 128
NTB = 4
ACT = 16
N_LAT = 4
N_TOK = 2


def active_plan(key):
    shards = N_LAT * N_TOK
    device_blocks = LAT_DEV // LATBLK
    cells = shards * CAP
    keys = jax.random.split(key, 6)
    local_scores = jax.random.randint(keys[0], (NTB, shards, device_blocks), 0, 1048576) * device_blocks + jnp.arange(device_blocks, dtype=jnp.int32)
    order = jnp.argsort(local_scores, axis=2, stable=True)[:, :, :CAP]
    cell_ids = (order + device_blocks * jnp.arange(shards, dtype=jnp.int32)[None, :, None]).reshape(NTB, cells)
    busy = jax.random.randint(keys[1], (NTB,), 0, shards)
    leaning = jax.random.randint(keys[2], (shards,), 0, 1048576)
    noise = jax.random.randint(keys[3], (NTB, cells), 0, 262144)
    owner = jnp.arange(cells, dtype=jnp.int32) // CAP
    score = noise + leaning[owner][None, :] + jnp.where(owner[None, :] == busy[:, None], 4194304, 0)
    score = score * cells + jnp.arange(cells, dtype=jnp.int32)[None, :]
    unused, picked = lax.top_k(score, ACT)
    block_ids = jnp.take_along_axis(cell_ids, picked, axis=1)
    counts = jax.random.randint(keys[4], (NTB,), ACT // 2, ACT + 1)
    fullest = jax.random.randint(keys[5], (), 0, NTB)
    places = jnp.arange(NTB, dtype=jnp.int32)
    counts = jnp.where(places == fullest, ACT, jnp.where(places == (fullest + 1) % NTB, ACT // 2, counts))
    return (block_ids.astype(jnp.int32), counts.astype(jnp.int32))


def draw_block_ids(key, part):
    return active_plan(key)[0]


def draw_counts(key, part):
    return active_plan(key)[1]


def levels(rng, dims, cuts, smallest, top_value):
    def one(axis_at, parts):
        draws = jax.random.uniform(jax.random.fold_in(jax.random.fold_in(rng, 6), axis_at), (parts,), jnp.float32, smallest / len(cuts), top_value / len(cuts))
        return jnp.repeat(jnp.exp(draws), dims[axis_at] // parts).reshape((-1,) + (1,) * (len(dims) - axis_at - 1))

    level = one(*cuts[0])
    for cut in cuts[1:]:
        level = level * one(*cut)
    return level


def centred(own_key, dims, deviation, reach, pieces=(), kind=jnp.bfloat16):
    gain = levels(own_key, dims, pieces, -0.22, 0.18) if pieces else 1.0
    array = jax.random.normal(own_key, dims, jnp.float32) * deviation * gain
    return jnp.minimum(jnp.maximum(array, -reach), reach).astype(kind)


def setup_inputs(seed: int = 0, part: int = 0) -> dict:
    key_of = jax.random.split(jax.random.key(seed), 8)
    part_splits = jax.random.split(jax.random.fold_in(key_of[7], part), 8)
    return {
        "tokens": centred(part_splits[0], (TOKENS, NL, D), 1.0, 6.0, ((0, 4), (1, 2))),
        "w_enc": centred(key_of[1], (NL, D, LAT), (D * NL) ** -0.5, 0.09375, ((0, 2), (2, 8))),
        "b_enc": centred(key_of[2], (LAT,), 0.5, 3.0, ((0, 8),), jnp.float32),
        "w_dec": centred(key_of[3], (NL, LAT, D), (ACT * 32) ** -0.5, 0.25, ((0, 2), (1, 8))),
        "b_dec": centred(key_of[4], (NL, D), 0.5, 3.0, ((0, 2),), jnp.float32),
        "block_ids": draw_block_ids(jax.random.fold_in(jax.random.fold_in(key_of[7], part), 71), part),
        "counts": draw_counts(jax.random.fold_in(jax.random.fold_in(key_of[7], part), 71), part),
    }


def reference(tokens, w_enc, b_enc, w_dec, b_dec, block_ids, counts):
    shards = N_LAT * N_TOK
    device_blocks = LAT_DEV // LATBLK
    enc_all = w_enc.reshape(NL, D, NBLK, LATBLK)
    dec_all = w_dec.reshape(NL, NBLK, LATBLK, D)
    bias_all = b_enc.reshape(NBLK, LATBLK)
    token_blocks = tokens.reshape(NTB, TBLK, NL, D)

    def one_block(args):
        token_block, picks, number = args
        live = jnp.arange(ACT, dtype=jnp.int32) < number
        enc_pick = jnp.take(enc_all, picks, axis=2).astype(jnp.float32)
        pre = jnp.einsum("tld,ldsk->tsk", token_block.astype(jnp.float32), enc_pick)
        pre = pre + jnp.take(bias_all, picks, axis=0)[None]
        codes = (jnp.maximum(pre, 0.0) * live.astype(jnp.float32)[None, :, None]).astype(jnp.bfloat16)
        dec_pick = jnp.take(dec_all, picks, axis=1).astype(jnp.float32)
        slot_terms = jnp.einsum("tsk,lskd->stld", codes.astype(jnp.float32), dec_pick)
        owner = ((picks // device_blocks)[:, None] == jnp.arange(shards, dtype=jnp.int32)[None, :]) & live[:, None]
        shard_terms = jnp.einsum("sn,stld->ntld", owner.astype(jnp.float32), slot_terms)
        rounded = lax.optimization_barrier(shard_terms.astype(jnp.bfloat16)).astype(jnp.float32)
        recon = jnp.sum(rounded, axis=0) + b_dec[None]
        residual = (recon - token_block.astype(jnp.float32)).astype(jnp.bfloat16)
        grad = jnp.einsum("tld,lskd->tsk", residual.astype(jnp.float32), dec_pick)
        contrib = jnp.sum(codes.astype(jnp.float32) * grad, axis=0)
        return residual, contrib

    residual, contrib = lax.map(one_block, (token_blocks, block_ids, counts))
    live_all = jnp.arange(ACT, dtype=jnp.int32)[None, :] < counts[:, None]
    onehot = ((block_ids[:, :, None] == jnp.arange(NBLK, dtype=jnp.int32)[None, None, :]) & live_all[:, :, None]).astype(jnp.float32)
    scale_grad = jnp.einsum("bsn,bsk->nk", onehot, contrib) / TBLK
    return residual.reshape(TOKENS, NL, D), scale_grad.reshape(LAT)
```

```python
import jax
import jax.numpy as jnp
from jax import lax
from jax.sharding import PartitionSpec as P

LATBLK = 64
TBLK = 128
CAP = 3
SLOT = CAP * LATBLK


def swap(value, axis, mask):
    size = lax.axis_size(axis)
    return lax.ppermute(value, axis, [(i, i ^ mask) for i in range(size)])


def masks_of(axis):
    size = lax.axis_size(axis)
    return [1 << i for i in range(size.bit_length() - 1)]


def spread(value):
    have = {0: value}
    for mask in reversed(masks_of("lat")):
        for offset in list(have):
            have[offset ^ mask] = swap(have[offset], "lat", mask)
    return have


def collect(parts):
    held = dict(parts)
    for mask in masks_of("lat"):
        for offset in sorted(held):
            if offset & mask:
                arrived = swap(held.pop(offset).astype(jnp.bfloat16), "lat", mask)
                held[offset ^ mask] = held[offset ^ mask] + arrived.astype(jnp.float32)
    return held[0]


def sum_layers(value):
    for mask in masks_of("layer"):
        total = value.astype(jnp.float32) + swap(value, "layer", mask).astype(jnp.float32)
        value = total.astype(value.dtype)
    return total


def on_device(tokens, w_enc, b_enc, w_dec, b_dec, block_ids, counts):
    own_rows, layers_here, width = tokens.shape
    assert own_rows == TBLK and layers_here == 1
    latents_here = w_enc.shape[2]
    device_blocks = latents_here // LATBLK
    slot_total = block_ids.shape[1]
    half = width // 2
    lat_size = lax.axis_size("lat")
    place = lax.axis_index("lat")
    core = lax.axis_index("tok")
    cycle_place = place * lax.axis_size("tok") + core
    bf16, f32 = jnp.bfloat16, jnp.float32

    order = place ^ jnp.arange(lat_size, dtype=jnp.int32)
    ids = jnp.take(block_ids, order, axis=0)
    live = jnp.arange(slot_total, dtype=jnp.int32)[None, :] < jnp.take(counts, order)[:, None]
    mine = live & (ids // device_blocks == cycle_place)
    position = jnp.cumsum(mine.astype(jnp.int32), axis=1) - 1
    select = mine[:, :, None] & (
        position[:, :, None] == jnp.arange(CAP, dtype=jnp.int32)[None, None, :]
    )
    pick = jnp.sum(select.astype(jnp.int32) * (ids % device_blocks + 1)[:, :, None], axis=1) - 1

    onehot = pick[:, :, None] == jnp.arange(device_blocks, dtype=jnp.int32)[None, None, :]
    column = (
        jnp.where(pick < 0, -latents_here, pick * LATBLK)[:, :, None]
        + jnp.arange(LATBLK, dtype=jnp.int32)[None, None, :]
    ).reshape(1, lat_size * SLOT)
    choose = (jnp.arange(latents_here, dtype=jnp.int32)[:, None] == column).astype(bf16)
    bias_own = jnp.sum(
        jnp.where(onehot[:, :, :, None], b_enc.reshape(1, 1, device_blocks, LATBLK), 0.0), axis=2
    ).reshape(lat_size, SLOT)

    def picked(a, b):
        return jnp.dot(a, b, preferred_element_type=f32).astype(bf16)

    enc_sel = picked(w_enc[0], choose)
    dec_sel = picked(choose.T, w_dec[0])

    def cut(value, axis, which):
        return lax.dynamic_slice_in_dim(value, which * half, half, axis)

    enc_two = (cut(enc_sel, 0, core), swap(cut(enc_sel, 0, 1 - core), "tok", 1))
    dec_two = (cut(dec_sel, 1, core), swap(cut(dec_sel, 1, 1 - core), "tok", 1))
    bias_two = (bias_own, swap(bias_own, "tok", 1))

    def slot(offset):
        return slice(offset * SLOT, (offset + 1) * SLOT)

    own = tokens.reshape(own_rows, width)
    own_half = cut(own, 1, core)
    token_blocks = spread(own_half)

    codes = {}
    parts = {}
    for offset in token_blocks:
        block = token_blocks[offset]
        part = jnp.stack(
            [jnp.dot(block, w[:, slot(offset)], preferred_element_type=f32) for w in enc_two]
        ).astype(bf16)
        other = swap(part, "tok", 1)
        both = (part.astype(f32) + other[::-1].astype(f32)).astype(bf16)
        pre = sum_layers(both) + jnp.stack([b[offset] for b in bias_two])[:, None, :]
        codes[offset] = jnp.maximum(pre, 0.0).astype(bf16)
        parts[offset] = sum(
            jnp.dot(codes[offset][i], dec_two[i][slot(offset)], preferred_element_type=f32)
            for i in range(2)
        )

    recon = collect(parts) + cut(b_dec, 1, core)
    residual_half = (recon - own_half.astype(f32)).astype(bf16)
    residual_other = swap(residual_half, "tok", 1)
    residual = jnp.where(
        core == 0,
        jnp.concatenate([residual_half, residual_other], axis=1),
        jnp.concatenate([residual_other, residual_half], axis=1),
    )

    error_blocks = spread(residual_half)
    contrib = []
    for offset in range(lat_size):
        grad = jnp.stack(
            [
                lax.dot_general(
                    error_blocks[offset],
                    w[slot(offset)],
                    (((1,), (1,)), ((), ())),
                    preferred_element_type=f32,
                )
                for w in dec_two
            ]
        )
        contrib.append(jnp.sum(codes[offset].astype(f32) * grad, axis=1))
    contrib = jnp.stack(contrib, axis=1)
    contrib = sum_layers(contrib[0] + swap(contrib[1], "tok", 1))
    scale_grad = jnp.sum(
        jnp.where(onehot[:, :, :, None], contrib.reshape(lat_size, CAP, 1, LATBLK), 0.0),
        axis=(0, 1),
    ) * (1.0 / TBLK)
    return residual.reshape(tokens.shape), scale_grad.reshape(latents_here)


def solution(mesh):
    in_specs = (
        P(("groups", "lat"), "layer", None),
        P("layer", None, ("lat", "tok")),
        P(("lat", "tok")),
        P("layer", ("lat", "tok"), None),
        P("layer", None),
        P("groups", None),
        P("groups"),
    )
    out_specs = (P(("groups", "lat"), "layer", None), P(("groups", "lat", "tok")))
    return jax.shard_map(
        on_device, mesh=mesh, in_specs=in_specs, out_specs=out_specs, check_vma=False
    )
```

```python
import jax
import jax.numpy as jnp
from jax import lax
from jax.experimental import pallas as pl
from jax.experimental.pallas import tpu as pltpu
from jax.sharding import PartitionSpec as P

LATBLK = 64
TBLK = 128
CAP = 3
SLOT = CAP * LATBLK


def swap(value, axis, mask):
    size = lax.axis_size(axis)
    return lax.ppermute(value, axis, [(i, i ^ mask) for i in range(size)])


def masks_of(axis):
    size = lax.axis_size(axis)
    return [1 << i for i in range(size.bit_length() - 1)]


def spread(value):
    have = {0: value}
    for mask in reversed(masks_of("lat")):
        for offset in list(have):
            have[offset ^ mask] = swap(have[offset], "lat", mask)
    return have


def collect(parts):
    held = dict(parts)
    for mask in masks_of("lat"):
        for offset in sorted(held):
            if offset & mask:
                arrived = swap(held.pop(offset).astype(jnp.bfloat16), "lat", mask)
                held[offset ^ mask] = held[offset ^ mask] + arrived.astype(jnp.float32)
    return held[0]


def sum_layers(value):
    for mask in masks_of("layer"):
        total = value.astype(jnp.float32) + swap(value, "layer", mask).astype(jnp.float32)
        value = total.astype(value.dtype)
    return total


def selected(w_enc, w_dec, pick, half_at):
    width, latents = w_enc.shape
    half = width // 2
    blocks = pick.shape[0] // CAP

    def body(pick_ref, half_ref, *refs):
        enc_refs, dec_refs, out_ref = refs[:CAP], refs[CAP : 2 * CAP], refs[2 * CAP]
        step = pl.program_id(0)
        row = lax.broadcasted_iota(jnp.int32, (LATBLK, 2 * LATBLK), 0)
        lane = lax.broadcasted_iota(jnp.int32, (LATBLK, 2 * LATBLK), 1)
        for s in range(CAP):
            odd = lax.rem(pick_ref[step * CAP + s], 2)
            choose = (lane == row + odd * LATBLK).astype(jnp.bfloat16)
            rows = slice(s * LATBLK, (s + 1) * LATBLK)
            out_ref[0, rows, :] = lax.dot_general(
                choose, enc_refs[s][...], (((1,), (1,)), ((), ())),
                preferred_element_type=jnp.float32,
            ).astype(jnp.bfloat16)
            out_ref[1, rows, :] = dec_refs[s][...]

    def enc_spec(s):
        return pl.BlockSpec(
            (half, 2 * LATBLK), lambda i, p, h: (h[0], lax.div(p[i * CAP + s], 2))
        )

    def dec_spec(s):
        return pl.BlockSpec((LATBLK, half), lambda i, p, h: (p[i * CAP + s], h[0]))

    return pl.pallas_call(
        body,
        grid_spec=pltpu.PrefetchScalarGridSpec(
            num_scalar_prefetch=2,
            grid=(blocks,),
            in_specs=[enc_spec(s) for s in range(CAP)] + [dec_spec(s) for s in range(CAP)],
            out_specs=pl.BlockSpec((2, SLOT, half), lambda i, p, h: (0, i, 0)),
        ),
        out_shape=jax.ShapeDtypeStruct((2, blocks * SLOT, half), jnp.bfloat16),
        compiler_params=pltpu.CompilerParams(vmem_limit_bytes=24 * 1024 * 1024),
        cost_estimate=pl.CostEstimate(
            flops=blocks * CAP * 2 * LATBLK * 2 * LATBLK * half,
            bytes_accessed=blocks * SLOT * half * 10,
            transcendentals=0,
        ),
    )(pick, half_at, *([w_enc] * CAP), *([w_dec] * CAP))


ROW_PARTS = 1


def on_device(tokens, w_enc, b_enc, w_dec, b_dec, block_ids, counts):
    own_rows, layers_here, width = tokens.shape
    assert own_rows == TBLK and layers_here == 1
    latents_here = w_enc.shape[2]
    device_blocks = latents_here // LATBLK
    slot_total = block_ids.shape[1]
    half = width // 2
    lat_size = lax.axis_size("lat")
    place = lax.axis_index("lat")
    core = lax.axis_index("tok")
    cycle_place = place * lax.axis_size("tok") + core
    bf16, f32 = jnp.bfloat16, jnp.float32

    def cut(value, axis, which):
        return lax.dynamic_slice_in_dim(value, which * half, half, axis)

    own_half = cut(tokens.reshape(own_rows, width), 1, core)
    rows = own_rows // ROW_PARTS
    own_parts = [own_half[r * rows : (r + 1) * rows] for r in range(ROW_PARTS)]
    token_blocks = [spread(part) for part in own_parts]

    order = place ^ jnp.arange(lat_size, dtype=jnp.int32)
    owner = order[:, None] == jnp.arange(lat_size, dtype=jnp.int32)[None, :]
    ids = jnp.sum(jnp.where(owner[:, :, None], block_ids[None], 0), axis=1)
    live_count = jnp.sum(jnp.where(owner, counts[None], 0), axis=1)
    live = jnp.arange(slot_total, dtype=jnp.int32)[None, :] < live_count[:, None]
    mine = live & (ids // device_blocks == cycle_place)
    position = jnp.cumsum(mine.astype(jnp.int32), axis=1) - 1
    select = mine[:, :, None] & (
        position[:, :, None] == jnp.arange(CAP, dtype=jnp.int32)[None, None, :]
    )
    pick = jnp.sum(select.astype(jnp.int32) * (ids % device_blocks + 1)[:, :, None], axis=1) - 1
    onehot = pick[:, :, None] == jnp.arange(device_blocks, dtype=jnp.int32)[None, None, :]
    bias_pick = jnp.sum(
        jnp.where(onehot[:, :, :, None], b_enc.reshape(1, 1, device_blocks, LATBLK), 0.0), axis=2
    )
    bias_own = jnp.where(pick[:, :, None] < 0, -jnp.inf, bias_pick).reshape(lat_size, SLOT)

    pick_flat = jnp.maximum(pick, 0).reshape(lat_size * CAP)
    sent = selected(w_enc[0], w_dec[0], pick_flat, jnp.full((1,), 1 - core, jnp.int32))
    held = selected(w_enc[0], w_dec[0], pick_flat, jnp.full((1,), core, jnp.int32))
    weights = (held, swap(sent, "tok", 1))
    bias_two = jnp.stack([bias_own, swap(bias_own, "tok", 1)])

    def slot(offset):
        return slice(offset * SLOT, (offset + 1) * SLOT)

    def times_rows(block, w):
        return lax.dot_general(
            block, w, (((1,), (1,)), ((), ())), preferred_element_type=f32
        )

    def forward(r):
        codes, parts = {}, {}
        for group in (range(lat_size - 1), range(lat_size - 1, lat_size)):
            part = jnp.stack(
                [
                    jnp.stack([times_rows(token_blocks[r][o], w[0, slot(o)]) for o in group])
                    for w in weights
                ]
            ).astype(bf16)
            other = swap(part, "tok", 1)
            both = (part.astype(f32) + other[::-1].astype(f32)).astype(bf16)
            pre = sum_layers(both) + bias_two[:, group.start : group.stop, None, :]
            code = jnp.maximum(pre, 0.0).astype(bf16)
            for at, o in enumerate(group):
                codes[o] = code[:, at]
                parts[o] = sum(
                    jnp.dot(code[i, at], weights[i][1, slot(o)], preferred_element_type=f32)
                    for i in range(2)
                )
        return codes, parts

    bias_dec = cut(b_dec, 1, core)
    codes, halves = [], []
    for r in range(ROW_PARTS):
        code, parts = forward(r)
        codes.append(code)
        recon = collect(parts) + bias_dec
        halves.append((recon - own_parts[r].astype(f32)).astype(bf16))

    contrib = 0.0
    for r in range(ROW_PARTS):
        error_blocks = spread(halves[r])
        contrib = contrib + jnp.stack(
            [
                jnp.stack(
                    [
                        jnp.sum(
                            codes[r][o][i].astype(f32)
                            * times_rows(error_blocks[o], weights[i][1, slot(o)]),
                            axis=0,
                        )
                        for o in range(lat_size)
                    ]
                )
                for i in range(2)
            ]
        )
    contrib = sum_layers(contrib[0] + swap(contrib[1], "tok", 1))
    scale_grad = jnp.sum(
        jnp.where(onehot[:, :, :, None], contrib.reshape(lat_size, CAP, 1, LATBLK), 0.0),
        axis=(0, 1),
    ) * (1.0 / TBLK)

    residual_half = jnp.concatenate(halves, axis=0)
    residual_other = swap(residual_half, "tok", 1)
    residual = jnp.where(
        core == 0,
        jnp.concatenate([residual_half, residual_other], axis=1),
        jnp.concatenate([residual_other, residual_half], axis=1),
    )
    return residual.reshape(tokens.shape), scale_grad.reshape(latents_here)


def solution(mesh):
    in_specs = (
        P(("groups", "lat"), "layer", None),
        P("layer", None, ("lat", "tok")),
        P(("lat", "tok")),
        P("layer", ("lat", "tok"), None),
        P("layer", None),
        P("groups", None),
        P("groups"),
    )
    out_specs = (P(("groups", "lat"), "layer", None), P(("groups", "lat", "tok")))
    return jax.shard_map(
        on_device, mesh=mesh, in_specs=in_specs, out_specs=out_specs, check_vma=False
    )
```

```python
import jax
import jax.numpy as jnp
from jax import lax
from jax.experimental import pallas as pl
from jax.experimental.pallas import tpu as pltpu
from jax.sharding import PartitionSpec as P

LATBLK = 64
TBLK = 128
CAP = 3
SLOT = CAP * LATBLK
ROW_PARTS = 2
PARAMS = pltpu.CompilerParams(vmem_limit_bytes=16 * 1024 * 1024)
SMALL = pl.CostEstimate(flops=0, bytes_accessed=0, transcendentals=0)


def swap(value, axis, mask):
    size = lax.axis_size(axis)
    return lax.ppermute(value, axis, [(i, i ^ mask) for i in range(size)])


def masks_of(axis):
    size = lax.axis_size(axis)
    return [1 << i for i in range(size.bit_length() - 1)]


def spread(value):
    have = {0: value}
    for mask in reversed(masks_of("lat")):
        for offset in list(have):
            have[offset ^ mask] = swap(have[offset], "lat", mask)
    return have


def sum_layers(value):
    for mask in masks_of("layer"):
        total = value.astype(jnp.float32) + swap(value, "layer", mask).astype(jnp.float32)
        value = total.astype(value.dtype)
    return total


def in_hbm(value):
    return pltpu.with_memory_space_constraint(value, pltpu.HBM)


def in_vmem(value):
    return pltpu.with_memory_space_constraint(value, pltpu.VMEM)


def half_of(tokens, core):
    rows, width = tokens.shape
    half = width // 2

    def body(core_ref, token_ref, out_ref):
        out_ref[...] = token_ref[...]

    return pl.pallas_call(
        body,
        grid_spec=pltpu.PrefetchScalarGridSpec(
            num_scalar_prefetch=1,
            grid=(1,),
            in_specs=[pl.BlockSpec((rows, half), lambda i, c: (0, c[0]))],
            out_specs=pl.BlockSpec((rows, half), lambda i, c: (0, 0)),
        ),
        out_shape=jax.ShapeDtypeStruct((rows, half), tokens.dtype),
        compiler_params=PARAMS,
        cost_estimate=SMALL,
    )(core, in_hbm(tokens))


def plan(block_ids, counts, places, bias):
    block_total, slot_total = block_ids.shape
    latents = bias.shape[0]
    device_blocks = latents // LATBLK
    wide = 2 * LATBLK

    def body(ids_ref, counts_ref, places_ref, bias_ref, own_ref, other_ref, out_ref):
        place, core = places_ref[0], places_ref[1]
        pick_refs = (own_ref, other_ref)
        for offset in range(block_total):
            block = place ^ offset
            for pick_ref in pick_refs:
                for s in range(CAP):
                    pick_ref[offset * CAP + s] = -1

            def step(slot, found):
                chosen = ids_ref[block, slot]
                shard = lax.div(chosen, device_blocks)
                local = lax.rem(chosen, device_blocks)
                live = slot < counts_ref[block]
                new = []
                for i, pick_ref in enumerate(pick_refs):
                    mine = live & (shard == place * 2 + (core ^ i))
                    at = offset * CAP + jnp.minimum(found[i], CAP - 1)

                    @pl.when(mine)
                    def _():
                        pick_ref[at] = local

                    new.append(found[i] + mine.astype(jnp.int32))
                return tuple(new)

            lax.fori_loop(0, slot_total, step, (jnp.int32(0), jnp.int32(0)))
        for offset in range(block_total):
            for s in range(CAP):
                chosen = own_ref[offset * CAP + s]
                at = jnp.maximum(chosen, 0)
                pair = bias_ref[pl.ds(lax.div(at, 2), 1), :]
                row = jnp.where(lax.rem(at, 2) == 1, pair[:, LATBLK:], pair[:, :LATBLK])
                out_ref[offset : offset + 1, s * LATBLK : (s + 1) * LATBLK] = jnp.where(
                    chosen < 0, -jnp.inf, row
                )

    smem = pl.BlockSpec(memory_space=pltpu.SMEM)
    picks = jax.ShapeDtypeStruct((block_total * CAP,), jnp.int32)
    return pl.pallas_call(
        body,
        grid=(1,),
        in_specs=[smem] * 3 + [whole((latents // wide, wide))],
        out_specs=[smem, smem, whole((block_total, SLOT))],
        out_shape=[picks, picks, jax.ShapeDtypeStruct((block_total, SLOT), jnp.float32)],
        compiler_params=PARAMS,
        cost_estimate=SMALL,
    )(in_hbm(block_ids), in_hbm(counts), places, in_hbm(bias.reshape(latents // wide, wide)))


def encoder_slots(w_enc, pick, core):
    half = w_enc.shape[0] // 2
    blocks = pick.shape[0] // CAP

    def body(pick_ref, core_ref, *refs):
        step = pl.program_id(0)
        for s in range(CAP):
            odd = lax.rem(jnp.maximum(pick_ref[step * CAP + s], 0), 2)
            wide = refs[s][...]
            left, right = wide[:, :LATBLK], wide[:, LATBLK:]
            refs[CAP][:, s * LATBLK : (s + 1) * LATBLK] = jnp.where(odd == 1, right, left)

    def spec(s):
        return pl.BlockSpec(
            (half, 2 * LATBLK),
            lambda i, p, c: (c[0], lax.div(jnp.maximum(p[i * CAP + s], 0), 2)),
        )

    return pl.pallas_call(
        body,
        grid_spec=pltpu.PrefetchScalarGridSpec(
            num_scalar_prefetch=2,
            grid=(blocks,),
            in_specs=[spec(s) for s in range(CAP)],
            out_specs=pl.BlockSpec((None, half, SLOT), lambda i, p, c: (i, 0, 0)),
        ),
        out_shape=jax.ShapeDtypeStruct((blocks, half, SLOT), jnp.bfloat16),
        compiler_params=PARAMS,
        cost_estimate=SMALL,
    )(pick, core, *([in_hbm(w_enc)] * CAP))


def decoder_slots(w_dec, pick, core):
    half = w_dec.shape[1] // 2
    blocks = pick.shape[0] // CAP

    def body(pick_ref, core_ref, *refs):
        for s in range(CAP):
            refs[CAP][s * LATBLK : (s + 1) * LATBLK, :] = refs[s][...]

    def spec(s):
        return pl.BlockSpec(
            (LATBLK, half), lambda i, p, c: (jnp.maximum(p[i * CAP + s], 0), c[0])
        )

    return pl.pallas_call(
        body,
        grid_spec=pltpu.PrefetchScalarGridSpec(
            num_scalar_prefetch=2,
            grid=(blocks,),
            in_specs=[spec(s) for s in range(CAP)],
            out_specs=pl.BlockSpec((None, SLOT, half), lambda i, p, c: (i, 0, 0)),
        ),
        out_shape=jax.ShapeDtypeStruct((blocks, SLOT, half), jnp.bfloat16),
        compiler_params=PARAMS,
        cost_estimate=SMALL,
    )(pick, core, *([in_hbm(w_dec)] * CAP))


def whole(shape):
    return pl.BlockSpec(shape, lambda i, *_: (0,) * len(shape))


def slot_specs(weights, offsets):
    return [
        pl.BlockSpec((None, *w.shape[1:]), lambda i, *_, o=o: (o, 0, 0))
        for o in offsets
        for w in weights
    ]


def slots(weights, offsets):
    return [w for _ in offsets for w in weights]


def across(a, b):
    return lax.dot_general(a, b, (((1,), (1,)), ((), ())), preferred_element_type=jnp.float32)


def encode(blocks, weights, offsets, core):
    count = len(blocks)
    rows, half = blocks[0].shape

    def body(core_ref, *refs):
        out_ref = refs[-1]
        first = core_ref[0] == 0
        for at in range(count):
            own, other = [
                jnp.dot(
                    refs[at][...], refs[count + 2 * at + i][...],
                    preferred_element_type=jnp.float32,
                ).astype(jnp.bfloat16)
                for i in range(2)
            ]
            out_ref[at, :, :SLOT] = jnp.where(first, own, other)
            out_ref[at, :, SLOT:] = jnp.where(first, other, own)

    return pl.pallas_call(
        body,
        grid_spec=pltpu.PrefetchScalarGridSpec(
            num_scalar_prefetch=1,
            grid=(1,),
            in_specs=[whole((rows, half))] * count + slot_specs(weights, offsets),
            out_specs=whole((count, rows, 2 * SLOT)),
        ),
        out_shape=jax.ShapeDtypeStruct((count, rows, 2 * SLOT), jnp.bfloat16),
        compiler_params=PARAMS,
        cost_estimate=SMALL,
    )(core, *[in_vmem(block) for block in blocks], *slots(weights, offsets))


def own_and_other(value, core_ref):
    low, high = value[:, :SLOT], value[:, SLOT:]
    first = core_ref[0] == 0
    return jnp.where(first, low, high), jnp.where(first, high, low)


def decode(pre, biases, weights, offsets, splits, core):
    count, rows, _ = pre.shape
    half = weights[0].shape[2]

    def body(core_ref, *refs):
        pre_ref, bias_refs, weight_refs = refs[0], refs[1:3], refs[3 : 3 + 2 * count]
        code_ref, part_refs = refs[3 + 2 * count], refs[4 + 2 * count :]
        for at, offset in enumerate(offsets):
            total = None
            for i, one in enumerate(own_and_other(pre_ref[at], core_ref)):
                code = jnp.maximum(one + bias_refs[i][offset : offset + 1, :], 0.0)
                code = code.astype(jnp.bfloat16)
                code_ref[at, :, i * SLOT : (i + 1) * SLOT] = code
                term = jnp.dot(
                    code, weight_refs[2 * at + i][...], preferred_element_type=jnp.float32
                )
                total = term if total is None else total + term
            step = rows // splits[at]
            for r in range(splits[at]):
                part_ref = part_refs[sum(splits[:at]) + r]
                part_ref[...] = total[r * step : (r + 1) * step].astype(part_ref.dtype)

    shapes = [
        jax.ShapeDtypeStruct((rows // split, half), jnp.bfloat16 if offset else jnp.float32)
        for offset, split in zip(offsets, splits)
        for _ in range(split)
    ]
    code, *parts = pl.pallas_call(
        body,
        grid_spec=pltpu.PrefetchScalarGridSpec(
            num_scalar_prefetch=1,
            grid=(1,),
            in_specs=[whole(pre.shape)]
            + [whole(bias.shape) for bias in biases]
            + slot_specs(weights, offsets),
            out_specs=[whole(pre.shape)] + [whole(shape.shape) for shape in shapes],
        ),
        out_shape=[jax.ShapeDtypeStruct(pre.shape, jnp.bfloat16)] + shapes,
        compiler_params=PARAMS,
        cost_estimate=SMALL,
    )(core, pre, *biases, *slots(weights, offsets))
    by_offset = {}
    for offset, split in zip(offsets, splits):
        by_offset[offset], parts = parts[:split], parts[split:]
    return code, by_offset


def remainder(part, arrived, bias, tokens, core, r, rows):
    half = part.shape[1]

    def body(core_ref, part_ref, bias_ref, token_ref, *refs):
        total = part_ref[...]
        for arrived_ref in refs[:-1]:
            total = total + arrived_ref[...].astype(jnp.float32)
        total = total + bias_ref[...]
        refs[-1][...] = (total - token_ref[...].astype(jnp.float32)).astype(jnp.bfloat16)

    def at_part(value):
        return pl.BlockSpec((rows, half), lambda i, c: (r if value.shape[0] > rows else 0, 0))

    return pl.pallas_call(
        body,
        grid_spec=pltpu.PrefetchScalarGridSpec(
            num_scalar_prefetch=1,
            grid=(1,),
            in_specs=[
                at_part(part),
                pl.BlockSpec((1, half), lambda i, c: (0, c[0])),
                at_part(tokens),
            ]
            + [at_part(value) for value in arrived],
            out_specs=pl.BlockSpec((rows, half), lambda i, c: (0, 0)),
        ),
        out_shape=jax.ShapeDtypeStruct((rows, half), jnp.bfloat16),
        compiler_params=PARAMS,
        cost_estimate=SMALL,
    )(core, part, bias, tokens, *arrived)


def gradient(error, codes, at, first, weights, offset):
    rows, half = error.shape

    def body(error_ref, code_ref, own_ref, other_ref, out_ref):
        for i, weight_ref in enumerate((own_ref, other_ref)):
            code = code_ref[:, i * SLOT : (i + 1) * SLOT].astype(jnp.float32)
            grad = across(error_ref[...], weight_ref[...])
            out_ref[i : i + 1, :] = jnp.sum(code * grad, axis=0, keepdims=True)

    return pl.pallas_call(
        body,
        grid=(1,),
        in_specs=[
            whole((rows, half)),
            pl.BlockSpec((None, rows, 2 * SLOT), lambda i: (at, first, 0)),
        ]
        + slot_specs(weights, [offset]),
        out_specs=whole((2, SLOT)),
        out_shape=jax.ShapeDtypeStruct((2, SLOT), jnp.float32),
        compiler_params=PARAMS,
        cost_estimate=SMALL,
    )(error, codes, *slots(weights, [offset]))


def gathered(terms):
    blocks = len(terms)
    flat = [term for block in terms for term in block]
    ends = [sum(len(block) for block in terms[: i + 1]) for i in range(blocks)]

    def body(*refs):
        for o in range(blocks):
            total = None
            for ref in refs[ends[o] - len(terms[o]) : ends[o]]:
                total = ref[...] if total is None else total + ref[...]
            for i in range(2):
                refs[len(flat) + i][o : o + 1, :] = total[i : i + 1, :]

    shape = jax.ShapeDtypeStruct((blocks, SLOT), jnp.float32)
    return pl.pallas_call(
        body,
        grid=(1,),
        in_specs=[whole((2, SLOT))] * len(flat),
        out_specs=[whole(shape.shape)] * 2,
        out_shape=[shape, shape],
        compiler_params=PARAMS,
        cost_estimate=SMALL,
    )(*flat)


def by_latent(total, pick, latents):
    wide = 2 * LATBLK
    blocks = total.shape[0]

    def body(pick_ref, total_ref, out_ref):
        out_ref[...] = jnp.zeros(out_ref.shape, jnp.float32)
        lane = lax.broadcasted_iota(jnp.int32, (1, wide), 1)
        for o in range(blocks):
            for s in range(CAP):
                chosen = pick_ref[o * CAP + s]
                at = jnp.maximum(chosen, 0)
                value = total_ref[o : o + 1, s * LATBLK : (s + 1) * LATBLK] * (1.0 / TBLK)
                here = (lane // LATBLK == lax.rem(at, 2)) & (chosen >= 0)
                row = pl.ds(lax.div(at, 2), 1)
                pair = jnp.concatenate([value, value], axis=1)
                out_ref[row, :] = out_ref[row, :] + jnp.where(here, pair, 0.0)

    return pl.pallas_call(
        body,
        grid_spec=pltpu.PrefetchScalarGridSpec(
            num_scalar_prefetch=1,
            grid=(1,),
            in_specs=[whole(total.shape)],
            out_specs=whole((latents // wide, wide)),
        ),
        out_shape=jax.ShapeDtypeStruct((latents // wide, wide), jnp.float32),
        compiler_params=PARAMS,
        cost_estimate=SMALL,
    )(pick, total).reshape(latents)


def side_by_side(own, other, core):
    parts = len(own)
    rows, half = own[0].shape

    def body(core_ref, *refs):
        out_ref = refs[-1]
        first = core_ref[0] == 0
        for r in range(parts):
            here, there = refs[r][...], refs[parts + r][...]
            at = slice(r * rows, (r + 1) * rows)
            out_ref[at, :half] = jnp.where(first, here, there)
            out_ref[at, half:] = jnp.where(first, there, here)

    return pl.pallas_call(
        body,
        grid_spec=pltpu.PrefetchScalarGridSpec(
            num_scalar_prefetch=1,
            grid=(1,),
            in_specs=[whole((rows, half))] * (2 * parts),
            out_specs=whole((parts * rows, 2 * half)),
        ),
        out_shape=jax.ShapeDtypeStruct((parts * rows, 2 * half), own[0].dtype),
        compiler_params=PARAMS,
        cost_estimate=SMALL,
    )(core, *own, *other)


def on_device(tokens, w_enc, b_enc, w_dec, b_dec, block_ids, counts):
    own_rows, layers_here, width = tokens.shape
    assert own_rows == TBLK and layers_here == 1
    latents_here = w_enc.shape[2]
    device_blocks = latents_here // LATBLK
    half = width // 2
    lat_size = lax.axis_size("lat")
    place = lax.axis_index("lat")
    core = lax.axis_index("tok")
    bf16, f32 = jnp.bfloat16, jnp.float32

    odds = list(range(1, lat_size, 2))
    evens = list(range(2, lat_size, 2))
    core_at = jnp.full((1,), core, jnp.int32)
    own_half = half_of(tokens.reshape(own_rows, width), core_at)
    near_tokens = swap(own_half, "lat", 1)

    own_pick, other_pick, bias_own = plan(
        block_ids, counts, jnp.stack([place, core]).astype(jnp.int32), b_enc
    )
    enc_own = encoder_slots(w_enc[0], own_pick, core_at)
    enc_swapped, near_tokens = lax.optimization_barrier((swap(w_enc, "tok", 1), near_tokens))
    enc_two = [enc_own, encoder_slots(enc_swapped[0], other_pick, core_at)]
    token_blocks = {0: own_half, 1: near_tokens}
    for mask in reversed(masks_of("lat")):
        if mask > 1:
            for offset in [o for o in token_blocks if o % 2 == 0]:
                token_blocks[offset ^ mask] = swap(token_blocks[offset], "lat", mask)
    even_tokens, enc_two = lax.optimization_barrier(
        ([token_blocks[o] for o in evens], enc_two)
    )
    for offset, value in zip(evens, even_tokens):
        token_blocks[offset] = value
        token_blocks[offset ^ 1] = swap(value, "lat", 1)
    biases = (bias_own, swap(bias_own, "tok", 1))

    def encoded(offsets):
        return encode([token_blocks[o] for o in offsets], enc_two, offsets, core_at)

    def forward(term, offsets, split):
        other = swap(term, "tok", 1)
        both = (term.astype(f32) + other.astype(f32)).astype(bf16)
        pre = sum_layers(both)
        code, parts = decode(
            pre, biases, dec_two, offsets, [split] * len(offsets), core_at
        )
        return {o: (code, at) for at, o in enumerate(offsets)}, parts

    dec_two = [
        decoder_slots(w_dec[0], own_pick, core_at),
        decoder_slots(swap(w_dec, "tok", 1)[0], other_pick, core_at),
    ]
    codes, parts = {}, {}
    for offsets, split in ((evens, 1), ([0, 1], 1), (odds[1:], ROW_PARTS)):
        code, part = forward(encoded(offsets), offsets, split)
        codes.update(code)
        parts.update(part)

    arrived = {
        o: [swap(part, "lat", o) for part in parts[o]] for o in [*evens, *odds]
    }
    halves = [
        remainder(
            parts[0][0],
            [value[r if len(value) > 1 else 0] for value in arrived.values()],
            b_dec,
            own_half,
            core_at,
            r,
            own_rows // ROW_PARTS,
        )
        for r in range(ROW_PARTS)
    ]

    terms = [[] for _ in range(lat_size)]
    for r in range(ROW_PARTS):
        for o, error in spread(halves[r]).items():
            terms[o].append(gradient(error, *codes[o], r, dec_two, o))
    own_sum, other_sum = gathered(terms)
    scale_grad = by_latent(
        sum_layers(own_sum + swap(other_sum, "tok", 1)), own_pick, latents_here
    )
    residual = side_by_side(halves, [swap(half, "tok", 1) for half in halves], core_at)
    return residual.reshape(tokens.shape), scale_grad


def solution(mesh):
    in_specs = (
        P(("groups", "lat"), "layer", None),
        P("layer", None, ("lat", "tok")),
        P(("lat", "tok")),
        P("layer", ("lat", "tok"), None),
        P("layer", None),
        P("groups", None),
        P("groups"),
    )
    out_specs = (P(("groups", "lat"), "layer", None), P(("groups", "lat", "tok")))
    return jax.shard_map(
        on_device, mesh=mesh, in_specs=in_specs, out_specs=out_specs, check_vma=False
    )
```

```python
import jax
import jax.numpy as jnp
from jax import lax
from jax.experimental import pallas as pl
from jax.experimental.pallas import tpu as pltpu
from jax.sharding import PartitionSpec as P

LATBLK = 64
TBLK = 128
CAP = 3
SLOT = CAP * LATBLK
ROW_PARTS = 2
PARAMS = pltpu.CompilerParams(vmem_limit_bytes=16 * 1024 * 1024)
SMALL = pl.CostEstimate(flops=0, bytes_accessed=0, transcendentals=0)


def swap(value, axis, mask):
    size = lax.axis_size(axis)
    return lax.ppermute(value, axis, [(i, i ^ mask) for i in range(size)])


def swap_both(value, mask):
    size = lax.axis_size("layer")
    pairs = [(2 * i + c, 2 * (i ^ mask) + 1 - c) for i in range(size) for c in range(2)]
    return lax.ppermute(value, ("layer", "tok"), pairs)


def masks_of(axis):
    size = lax.axis_size(axis)
    return [1 << i for i in range(size.bit_length() - 1)]


def sum_layers(value):
    for mask in masks_of("layer"):
        total = value.astype(jnp.float32) + swap(value, "layer", mask).astype(jnp.float32)
        value = total.astype(value.dtype)
    return total


def in_hbm(value):
    return pltpu.with_memory_space_constraint(value, pltpu.HBM)


def in_vmem(value):
    return pltpu.with_memory_space_constraint(value, pltpu.VMEM)


def half_of(tokens, core):
    rows, width = tokens.shape
    half = width // 2

    def body(core_ref, token_ref, out_ref):
        out_ref[...] = token_ref[...]

    return pl.pallas_call(
        body,
        grid_spec=pltpu.PrefetchScalarGridSpec(
            num_scalar_prefetch=1,
            grid=(1,),
            in_specs=[pl.BlockSpec((rows, half), lambda i, c: (0, c[0]))],
            out_specs=pl.BlockSpec((rows, half), lambda i, c: (0, 0)),
        ),
        out_shape=jax.ShapeDtypeStruct((rows, half), tokens.dtype),
        compiler_params=PARAMS,
        cost_estimate=SMALL,
    )(core, in_hbm(tokens))


def plan(block_ids, counts, places, bias):
    block_total, slot_total = block_ids.shape
    latents = bias.shape[0]
    device_blocks = latents // LATBLK
    wide = 2 * LATBLK
    shift = device_blocks.bit_length() - 1
    assert device_blocks == 1 << shift

    def body(ids_ref, counts_ref, places_ref, bias_ref, own_ref, other_ref, out_ref):
        place, core = places_ref[0], places_ref[1]
        pick_refs = (own_ref, other_ref)
        for offset in range(block_total):
            block = place ^ offset
            for pick_ref in pick_refs:
                for s in range(CAP):
                    pick_ref[offset * CAP + s] = -1

            def step(slot, found):
                chosen = ids_ref[block, slot]
                shard = lax.shift_right_logical(chosen, shift)
                local = chosen & (device_blocks - 1)
                live = slot < counts_ref[block]
                new = []
                for i, pick_ref in enumerate(pick_refs):
                    mine = live & (shard == place * 2 + (core ^ i))
                    at = offset * CAP + jnp.minimum(found[i], CAP - 1)

                    @pl.when(mine)
                    def _():
                        pick_ref[at] = local

                    new.append(found[i] + mine.astype(jnp.int32))
                return tuple(new)

            lax.fori_loop(0, slot_total, step, (jnp.int32(0), jnp.int32(0)), unroll=8)
        for offset in range(block_total):
            for s in range(CAP):
                chosen = own_ref[offset * CAP + s]
                at = jnp.maximum(chosen, 0)
                pair = bias_ref[pl.ds(lax.div(at, 2), 1), :]
                row = jnp.where(lax.rem(at, 2) == 1, pair[:, LATBLK:], pair[:, :LATBLK])
                out_ref[offset : offset + 1, s * LATBLK : (s + 1) * LATBLK] = jnp.where(
                    chosen < 0, -jnp.inf, row
                )

    smem = pl.BlockSpec(memory_space=pltpu.SMEM)
    picks = jax.ShapeDtypeStruct((block_total * CAP,), jnp.int32)
    return pl.pallas_call(
        body,
        grid=(1,),
        in_specs=[smem] * 3 + [whole((latents // wide, wide))],
        out_specs=[smem, smem, whole((block_total, SLOT))],
        out_shape=[picks, picks, jax.ShapeDtypeStruct((block_total, SLOT), jnp.float32)],
        compiler_params=PARAMS,
        cost_estimate=SMALL,
    )(in_hbm(block_ids), in_hbm(counts), places, in_hbm(bias.reshape(latents // wide, wide)))


def encoder_slots(w_enc, pick, core):
    half = w_enc.shape[0] // 2
    blocks = pick.shape[0] // CAP

    def body(pick_ref, core_ref, *refs):
        step = pl.program_id(0)
        placed = []
        for s in range(CAP):
            odd = lax.rem(jnp.maximum(pick_ref[step * CAP + s], 0), 2)
            wide = refs[s][...]
            turned = jnp.concatenate([wide[:, LATBLK:], wide[:, :LATBLK]], axis=1)
            placed.append(jnp.where(odd == s % 2, wide, turned))
        low = lax.broadcasted_iota(jnp.int32, placed[0].shape, 1) < LATBLK
        for s in range(0, CAP - 1, 2):
            refs[CAP][:, s * LATBLK : (s + 2) * LATBLK] = jnp.where(
                low, placed[s], placed[s + 1]
            )
        if CAP % 2:
            refs[CAP][:, (CAP - 1) * LATBLK :] = placed[-1][:, :LATBLK]

    def spec(s):
        return pl.BlockSpec(
            (half, 2 * LATBLK),
            lambda i, p, c: (c[0], lax.div(jnp.maximum(p[i * CAP + s], 0), 2)),
        )

    return pl.pallas_call(
        body,
        grid_spec=pltpu.PrefetchScalarGridSpec(
            num_scalar_prefetch=2,
            grid=(blocks,),
            in_specs=[spec(s) for s in range(CAP)],
            out_specs=pl.BlockSpec((None, half, SLOT), lambda i, p, c: (i, 0, 0)),
        ),
        out_shape=jax.ShapeDtypeStruct((blocks, half, SLOT), jnp.bfloat16),
        compiler_params=PARAMS,
        cost_estimate=SMALL,
    )(pick, core, *([in_hbm(w_enc)] * CAP))


def decoder_slots(w_dec, pick, core):
    half = w_dec.shape[1] // 2
    blocks = pick.shape[0] // CAP

    def body(pick_ref, core_ref, *refs):
        for s in range(CAP):
            refs[CAP][s * LATBLK : (s + 1) * LATBLK, :] = refs[s][...]

    def spec(s):
        return pl.BlockSpec(
            (LATBLK, half), lambda i, p, c: (jnp.maximum(p[i * CAP + s], 0), c[0])
        )

    return pl.pallas_call(
        body,
        grid_spec=pltpu.PrefetchScalarGridSpec(
            num_scalar_prefetch=2,
            grid=(blocks,),
            in_specs=[spec(s) for s in range(CAP)],
            out_specs=pl.BlockSpec((None, SLOT, half), lambda i, p, c: (i, 0, 0)),
        ),
        out_shape=jax.ShapeDtypeStruct((blocks, SLOT, half), jnp.bfloat16),
        compiler_params=PARAMS,
        cost_estimate=SMALL,
    )(pick, core, *([in_hbm(w_dec)] * CAP))


def whole(shape):
    return pl.BlockSpec(shape, lambda i, *_: (0,) * len(shape))


def slot_specs(weights, offsets):
    return [
        pl.BlockSpec((None, *w.shape[1:]), lambda i, *_, o=o: (o, 0, 0))
        for o in offsets
        for w in weights
    ]


def slots(weights, offsets):
    return [w for _ in offsets for w in weights]


def across(a, b):
    return lax.dot_general(a, b, (((1,), (1,)), ((), ())), preferred_element_type=jnp.float32)


def encode(blocks, weights, offsets, core):
    count = len(blocks)
    rows, half = blocks[0].shape

    def body(core_ref, *refs):
        out_ref = refs[-1]
        first = core_ref[0] == 0
        for at in range(count):
            own, other = [
                jnp.dot(
                    refs[at][...], refs[count + 2 * at + i][...],
                    preferred_element_type=jnp.float32,
                ).astype(jnp.bfloat16)
                for i in range(2)
            ]
            out_ref[at, :, :SLOT] = jnp.where(first, own, other)
            out_ref[at, :, SLOT:] = jnp.where(first, other, own)

    return pl.pallas_call(
        body,
        grid_spec=pltpu.PrefetchScalarGridSpec(
            num_scalar_prefetch=1,
            grid=(1,),
            in_specs=[whole((rows, half))] * count + slot_specs(weights, offsets),
            out_specs=whole((count, rows, 2 * SLOT)),
        ),
        out_shape=jax.ShapeDtypeStruct((count, rows, 2 * SLOT), jnp.bfloat16),
        compiler_params=PARAMS,
        cost_estimate=SMALL,
    )(core, *[in_vmem(block) for block in blocks], *slots(weights, offsets))


def own_and_other(value, core_ref):
    low, high = value[:, :SLOT], value[:, SLOT:]
    first = core_ref[0] == 0
    return jnp.where(first, low, high), jnp.where(first, high, low)


def decode(pre, biases, weights, offsets, splits, core):
    count, rows, _ = pre.shape
    half = weights[0].shape[2]

    def body(core_ref, *refs):
        pre_ref, bias_refs, weight_refs = refs[0], refs[1:3], refs[3 : 3 + 2 * count]
        code_ref, part_refs = refs[3 + 2 * count], refs[4 + 2 * count :]
        for at, offset in enumerate(offsets):
            total = None
            for i, one in enumerate(own_and_other(pre_ref[at], core_ref)):
                code = jnp.maximum(one + bias_refs[i][offset : offset + 1, :], 0.0)
                code = code.astype(jnp.bfloat16)
                code_ref[at, :, i * SLOT : (i + 1) * SLOT] = code
                term = jnp.dot(
                    code, weight_refs[2 * at + i][...], preferred_element_type=jnp.float32
                )
                total = term if total is None else total + term
            step = rows // splits[at]
            for r in range(splits[at]):
                part_ref = part_refs[sum(splits[:at]) + r]
                part_ref[...] = total[r * step : (r + 1) * step].astype(part_ref.dtype)

    shapes = [
        jax.ShapeDtypeStruct((rows // split, half), jnp.bfloat16 if offset % 2 else jnp.float32)
        for offset, split in zip(offsets, splits)
        for _ in range(split)
    ]
    code, *parts = pl.pallas_call(
        body,
        grid_spec=pltpu.PrefetchScalarGridSpec(
            num_scalar_prefetch=1,
            grid=(1,),
            in_specs=[whole(pre.shape)]
            + [whole(bias.shape) for bias in biases]
            + slot_specs(weights, offsets),
            out_specs=[whole(pre.shape)] + [whole(shape.shape) for shape in shapes],
        ),
        out_shape=[jax.ShapeDtypeStruct(pre.shape, jnp.bfloat16)] + shapes,
        compiler_params=PARAMS,
        cost_estimate=SMALL,
    )(core, pre, *biases, *slots(weights, offsets))
    by_offset = {}
    for offset, split in zip(offsets, splits):
        by_offset[offset], parts = parts[:split], parts[split:]
    return code, by_offset


def added(part, arrived):
    def body(part_ref, arrived_ref, out_ref):
        total = part_ref[...].astype(jnp.float32) + arrived_ref[...].astype(jnp.float32)
        out_ref[...] = total.astype(jnp.bfloat16)

    return pl.pallas_call(
        body,
        grid=(1,),
        in_specs=[whole(part.shape)] * 2,
        out_specs=whole(part.shape),
        out_shape=jax.ShapeDtypeStruct(part.shape, jnp.bfloat16),
        compiler_params=PARAMS,
        cost_estimate=SMALL,
    )(part, arrived)


def remainder(part, arrived, bias, tokens, core, r, rows):
    half = part.shape[1]

    def body(core_ref, part_ref, bias_ref, token_ref, *refs):
        total = part_ref[...]
        for arrived_ref in refs[:-1]:
            total = total + arrived_ref[...].astype(jnp.float32)
        total = total + bias_ref[...]
        refs[-1][...] = (total - token_ref[...].astype(jnp.float32)).astype(jnp.bfloat16)

    def at_part(value):
        return pl.BlockSpec((rows, half), lambda i, c: (r if value.shape[0] > rows else 0, 0))

    return pl.pallas_call(
        body,
        grid_spec=pltpu.PrefetchScalarGridSpec(
            num_scalar_prefetch=1,
            grid=(1,),
            in_specs=[
                at_part(part),
                pl.BlockSpec((1, half), lambda i, c: (0, c[0])),
                at_part(tokens),
            ]
            + [at_part(value) for value in arrived],
            out_specs=pl.BlockSpec((rows, half), lambda i, c: (0, 0)),
        ),
        out_shape=jax.ShapeDtypeStruct((rows, half), jnp.bfloat16),
        compiler_params=PARAMS,
        cost_estimate=SMALL,
    )(core, part, bias, tokens, *arrived)


def gradient(error, codes, at, first, weights, offset):
    rows, half = error.shape

    def body(error_ref, code_ref, own_ref, other_ref, out_ref):
        for i, weight_ref in enumerate((own_ref, other_ref)):
            code = code_ref[:, i * SLOT : (i + 1) * SLOT].astype(jnp.float32)
            grad = across(error_ref[...], weight_ref[...])
            out_ref[i : i + 1, :] = jnp.sum(code * grad, axis=0, keepdims=True)

    return pl.pallas_call(
        body,
        grid=(1,),
        in_specs=[
            whole((rows, half)),
            pl.BlockSpec((None, rows, 2 * SLOT), lambda i: (at, first, 0)),
        ]
        + slot_specs(weights, [offset]),
        out_specs=whole((2, SLOT)),
        out_shape=jax.ShapeDtypeStruct((2, SLOT), jnp.float32),
        compiler_params=PARAMS,
        cost_estimate=SMALL,
    )(error, codes, *slots(weights, [offset]))


def gathered(terms):
    blocks = len(terms)
    flat = [term for block in terms for term in block]
    ends = [sum(len(block) for block in terms[: i + 1]) for i in range(blocks)]

    def body(*refs):
        for o in range(blocks):
            total = None
            for ref in refs[ends[o] - len(terms[o]) : ends[o]]:
                total = ref[...] if total is None else total + ref[...]
            for i in range(2):
                refs[len(flat) + i][o : o + 1, :] = total[i : i + 1, :]

    shape = jax.ShapeDtypeStruct((blocks, SLOT), jnp.float32)
    return pl.pallas_call(
        body,
        grid=(1,),
        in_specs=[whole((2, SLOT))] * len(flat),
        out_specs=[whole(shape.shape)] * 2,
        out_shape=[shape, shape],
        compiler_params=PARAMS,
        cost_estimate=SMALL,
    )(*flat)


def by_latent(total, pick, latents):
    wide = 2 * LATBLK
    blocks = total.shape[0]

    def body(pick_ref, total_ref, out_ref):
        out_ref[...] = jnp.zeros(out_ref.shape, jnp.float32)
        lane = lax.broadcasted_iota(jnp.int32, (1, wide), 1)
        for o in range(blocks):
            for s in range(CAP):
                chosen = pick_ref[o * CAP + s]
                at = jnp.maximum(chosen, 0)
                value = total_ref[o : o + 1, s * LATBLK : (s + 1) * LATBLK] * (1.0 / TBLK)
                here = (lane // LATBLK == lax.rem(at, 2)) & (chosen >= 0)
                row = pl.ds(lax.div(at, 2), 1)
                pair = jnp.concatenate([value, value], axis=1)
                out_ref[row, :] = out_ref[row, :] + jnp.where(here, pair, 0.0)

    return pl.pallas_call(
        body,
        grid_spec=pltpu.PrefetchScalarGridSpec(
            num_scalar_prefetch=1,
            grid=(1,),
            in_specs=[whole(total.shape)],
            out_specs=whole((latents // wide, wide)),
        ),
        out_shape=jax.ShapeDtypeStruct((latents // wide, wide), jnp.float32),
        compiler_params=PARAMS,
        cost_estimate=SMALL,
    )(pick, total).reshape(latents)


def side_by_side(own, other, core):
    parts = len(own)
    rows, half = own[0].shape

    def body(core_ref, *refs):
        out_ref = refs[-1]
        first = core_ref[0] == 0
        for r in range(parts):
            here, there = refs[r][...], refs[parts + r][...]
            at = slice(r * rows, (r + 1) * rows)
            out_ref[at, :half] = jnp.where(first, here, there)
            out_ref[at, half:] = jnp.where(first, there, here)

    return pl.pallas_call(
        body,
        grid_spec=pltpu.PrefetchScalarGridSpec(
            num_scalar_prefetch=1,
            grid=(1,),
            in_specs=[whole((rows, half))] * (2 * parts),
            out_specs=whole((parts * rows, 2 * half)),
        ),
        out_shape=jax.ShapeDtypeStruct((parts * rows, 2 * half), own[0].dtype),
        compiler_params=PARAMS,
        cost_estimate=SMALL,
    )(core, *own, *other)


def on_device(tokens, w_enc, b_enc, w_dec, b_dec, block_ids, counts):
    own_rows, layers_here, width = tokens.shape
    assert own_rows == TBLK and layers_here == 1
    latents_here = w_enc.shape[2]
    device_blocks = latents_here // LATBLK
    half = width // 2
    lat_size = lax.axis_size("lat")
    place = lax.axis_index("lat")
    core = lax.axis_index("tok")
    bf16, f32 = jnp.bfloat16, jnp.float32

    odds = list(range(1, lat_size, 2))
    evens = list(range(2, lat_size, 2))
    core_at = jnp.full((1,), core, jnp.int32)
    own_half = half_of(tokens.reshape(own_rows, width), core_at)
    near_tokens = swap(own_half, "lat", 1)

    own_pick, other_pick, bias_own = plan(
        block_ids, counts, jnp.stack([place, core]).astype(jnp.int32), b_enc
    )
    enc_two = [
        encoder_slots(w_enc[0], own_pick, core_at),
        encoder_slots(swap(w_enc, "tok", 1)[0], other_pick, core_at),
    ]
    dec_own = decoder_slots(w_dec[0], own_pick, core_at)
    biases = (bias_own, swap(bias_own, "tok", 1))
    token_blocks = {0: own_half, 1: swap(own_half, "lat", 1)}
    for mask in reversed(masks_of("lat")):
        if mask > 1:
            for offset in [o for o in token_blocks if o % 2 == 0]:
                token_blocks[offset ^ mask] = swap(token_blocks[offset], "lat", mask)
    even_tokens, enc_two, dec_own, biases = lax.optimization_barrier(
        ([token_blocks[o] for o in evens], enc_two, dec_own, biases)
    )
    for offset, value in zip(evens, even_tokens):
        token_blocks[offset] = value
        token_blocks[offset ^ 1] = swap(value, "lat", 1)

    def encoded(offsets):
        return encode([token_blocks[o] for o in offsets], enc_two, offsets, core_at)

    def both_cores(term, other):
        return (term.astype(f32) + other.astype(f32)).astype(bf16)

    def summed(term, other):
        return sum_layers(both_cores(term, other))

    def forward(pre, offsets, splits):
        return decode(pre, biases, dec_two, offsets, splits, core_at)

    first, far = [*evens, 1], odds[1:]
    own_term, first_term = encoded([0]), encoded(first)
    first_other = swap(first_term, "tok", 1)
    w_dec_other, first_other = lax.optimization_barrier((swap(w_dec, "tok", 1), first_other))
    dec_two = [dec_own, decoder_slots(w_dec_other[0], other_pick, core_at)]
    far_tokens, dec_two = lax.optimization_barrier(([token_blocks[o] for o in far], dec_two))
    token_blocks.update(zip(far, far_tokens))
    first_code, first_parts = forward(
        summed(first_term, first_other), first, [ROW_PARTS] * len(evens) + [1]
    )
    far_term = encoded(far)
    far_sum = summed(far_term, swap(far_term, "tok", 1))
    far_code, far_parts = forward(far_sum, far, [ROW_PARTS] * len(far))

    far_sums = [{o - 1: swap(far_parts[o][r], "lat", 1) for o in far} for r in range(ROW_PARTS)]
    own_both = both_cores(own_term, swap(own_term, "tok", 1))
    own_both, near_part, far_sums[0] = lax.optimization_barrier(
        (own_both, first_parts[1][0], far_sums[0])
    )
    near_sum = swap(near_part, "lat", 1)
    own_code, own_parts = forward(sum_layers(own_both), [0], [1])
    codes = {
        o: (code, at)
        for code, offsets in ((first_code, first), (far_code, far), (own_code, [0]))
        for at, o in enumerate(offsets)
    }
    halves = []
    for r in range(ROW_PARTS):
        arrived = [near_sum]
        held = {o: added(first_parts[o][r], far_sums[r][o]) for o in evens}
        for mask in masks_of("lat")[1:]:
            for o in sorted(held):
                if o & mask:
                    value = swap(held.pop(o), "lat", mask)
                    if o == mask:
                        arrived.append(value)
                    else:
                        held[o ^ mask] = added(held[o ^ mask], value)
        halves.append(
            remainder(
                own_parts[0][0], arrived, b_dec, own_half, core_at, r, own_rows // ROW_PARTS
            )
        )

    terms = [[] for _ in range(lat_size)]
    before = None
    for r in range(ROW_PARTS):
        errors = {0: halves[r]}
        for mask in reversed(masks_of("lat")):
            sources = dict(errors)
            if mask == 1:
                errors[1] = swap(sources.pop(0), "lat", 1)
                last = max(sources)
                sources[last], errors[1], before = lax.optimization_barrier(
                    (sources[last], errors[1], before)
                )
            for o, error in sources.items():
                errors[o ^ mask] = swap(error, "lat", mask)
        before = errors[lat_size - 1]
        for o, error in errors.items():
            terms[o].append(gradient(error, *codes[o], r, dec_two, o))
    own_sum, other_sum = gathered(terms)
    total = own_sum + swap(other_sum, "tok", 1)
    for mask in range(1, lax.axis_size("layer")):
        total = total + swap(own_sum, "layer", mask) + swap_both(other_sum, mask)
    scale_grad = by_latent(total, own_pick, latents_here)
    residual = side_by_side(halves, [swap(half, "tok", 1) for half in halves], core_at)
    return residual.reshape(tokens.shape), scale_grad


def solution(mesh):
    in_specs = (
        P(("groups", "lat"), "layer", None),
        P("layer", None, ("lat", "tok")),
        P(("lat", "tok")),
        P("layer", ("lat", "tok"), None),
        P("layer", None),
        P("groups", None),
        P("groups"),
    )
    out_specs = (P(("groups", "lat"), "layer", None), P(("groups", "lat", "tok")))
    return jax.shard_map(
        on_device, mesh=mesh, in_specs=in_specs, out_specs=out_specs, check_vma=False
    )
```

```python
import jax
import jax.numpy as jnp
from jax import lax
from jax.experimental import pallas as pl
from jax.experimental.pallas import tpu as pltpu
from jax.sharding import PartitionSpec as P

LATBLK = 64
TBLK = 128
CAP = 3
SLOT = CAP * LATBLK
ROW_PARTS = 2
PARAMS = pltpu.CompilerParams(vmem_limit_bytes=16 * 1024 * 1024)
SMALL = pl.CostEstimate(flops=0, bytes_accessed=0, transcendentals=0)
AHEAD = pl.CostEstimate(flops=4000000000, bytes_accessed=0, transcendentals=0)


def swap(value, axis, mask):
    size = lax.axis_size(axis)
    return lax.ppermute(value, axis, [(i, i ^ mask) for i in range(size)])


def swap_both(value, mask):
    size = lax.axis_size("layer")
    pairs = [(2 * i + c, 2 * (i ^ mask) + 1 - c) for i in range(size) for c in range(2)]
    return lax.ppermute(value, ("layer", "tok"), pairs)


def masks_of(axis):
    size = lax.axis_size(axis)
    return [1 << i for i in range(size.bit_length() - 1)]


def sum_layers(value):
    for mask in masks_of("layer"):
        total = value.astype(jnp.float32) + swap(value, "layer", mask).astype(jnp.float32)
        value = total.astype(value.dtype)
    return total


def in_hbm(value):
    return pltpu.with_memory_space_constraint(value, pltpu.HBM)


def in_vmem(value):
    return pltpu.with_memory_space_constraint(value, pltpu.VMEM)


def half_of(tokens, core):
    rows, width = tokens.shape
    half = width // 2

    def body(core_ref, token_ref, out_ref):
        out_ref[...] = token_ref[...]

    return pl.pallas_call(
        body,
        grid_spec=pltpu.PrefetchScalarGridSpec(
            num_scalar_prefetch=1,
            grid=(1,),
            in_specs=[pl.BlockSpec((rows, half), lambda i, c: (0, c[0]))],
            out_specs=pl.BlockSpec((rows, half), lambda i, c: (0, 0)),
        ),
        out_shape=jax.ShapeDtypeStruct((rows, half), tokens.dtype),
        compiler_params=PARAMS,
        cost_estimate=SMALL,
    )(core, in_hbm(tokens))


def plan(block_ids, counts, places, bias):
    block_total, slot_total = block_ids.shape
    latents = bias.shape[0]
    device_blocks = latents // LATBLK
    wide = 2 * LATBLK
    shift = device_blocks.bit_length() - 1
    assert device_blocks == 1 << shift

    def body(ids_ref, counts_ref, places_ref, bias_ref, own_ref, other_ref, out_ref):
        place, core = places_ref[0], places_ref[1]
        pick_refs = (own_ref, other_ref)
        for offset in range(block_total):
            block = place ^ offset
            for pick_ref in pick_refs:
                for s in range(CAP):
                    pick_ref[offset * CAP + s] = -1

            def step(slot, found):
                chosen = ids_ref[block, slot]
                shard = lax.shift_right_logical(chosen, shift)
                local = chosen & (device_blocks - 1)
                live = slot < counts_ref[block]
                new = []
                for i, pick_ref in enumerate(pick_refs):
                    mine = live & (shard == place * 2 + (core ^ i))
                    at = offset * CAP + jnp.minimum(found[i], CAP - 1)

                    @pl.when(mine)
                    def _():
                        pick_ref[at] = local

                    new.append(found[i] + mine.astype(jnp.int32))
                return tuple(new)

            lax.fori_loop(0, slot_total, step, (jnp.int32(0), jnp.int32(0)), unroll=8)
        for offset in range(block_total):
            for s in range(CAP):
                chosen = own_ref[offset * CAP + s]
                at = jnp.maximum(chosen, 0)
                pair = bias_ref[pl.ds(lax.div(at, 2), 1), :]
                row = jnp.where(lax.rem(at, 2) == 1, pair[:, LATBLK:], pair[:, :LATBLK])
                out_ref[offset : offset + 1, s * LATBLK : (s + 1) * LATBLK] = jnp.where(
                    chosen < 0, -jnp.inf, row
                )

    smem = pl.BlockSpec(memory_space=pltpu.SMEM)
    picks = jax.ShapeDtypeStruct((block_total * CAP,), jnp.int32)
    return pl.pallas_call(
        body,
        grid=(1,),
        in_specs=[smem] * 3 + [whole((latents // wide, wide))],
        out_specs=[smem, smem, whole((block_total, SLOT))],
        out_shape=[picks, picks, jax.ShapeDtypeStruct((block_total, SLOT), jnp.float32)],
        compiler_params=PARAMS,
        cost_estimate=SMALL,
    )(in_hbm(block_ids), in_hbm(counts), places, in_hbm(bias.reshape(latents // wide, wide)))


def encoder_slots(w_enc, pick, core):
    half = w_enc.shape[0] // 2
    blocks = pick.shape[0] // CAP

    def body(pick_ref, core_ref, *refs):
        step = pl.program_id(0)
        placed = []
        for s in range(CAP):
            odd = lax.rem(jnp.maximum(pick_ref[step * CAP + s], 0), 2)
            wide = refs[s][...]
            turned = jnp.concatenate([wide[:, LATBLK:], wide[:, :LATBLK]], axis=1)
            placed.append(jnp.where(odd == s % 2, wide, turned))
        low = lax.broadcasted_iota(jnp.int32, placed[0].shape, 1) < LATBLK
        for s in range(0, CAP - 1, 2):
            refs[CAP][:, s * LATBLK : (s + 2) * LATBLK] = jnp.where(
                low, placed[s], placed[s + 1]
            )
        if CAP % 2:
            refs[CAP][:, (CAP - 1) * LATBLK :] = placed[-1][:, :LATBLK]

    def spec(s):
        return pl.BlockSpec(
            (half, 2 * LATBLK),
            lambda i, p, c: (c[0], lax.div(jnp.maximum(p[i * CAP + s], 0), 2)),
        )

    return pl.pallas_call(
        body,
        grid_spec=pltpu.PrefetchScalarGridSpec(
            num_scalar_prefetch=2,
            grid=(blocks,),
            in_specs=[spec(s) for s in range(CAP)],
            out_specs=pl.BlockSpec((None, half, SLOT), lambda i, p, c: (i, 0, 0)),
        ),
        out_shape=jax.ShapeDtypeStruct((blocks, half, SLOT), jnp.bfloat16),
        compiler_params=PARAMS,
        cost_estimate=SMALL,
    )(pick, core, *([in_hbm(w_enc)] * CAP))


def decoder_slots(w_dec, pick, core):
    half = w_dec.shape[1] // 2
    blocks = pick.shape[0] // CAP

    def body(pick_ref, core_ref, *refs):
        for s in range(CAP):
            refs[CAP][s * LATBLK : (s + 1) * LATBLK, :] = refs[s][...]

    def spec(s):
        return pl.BlockSpec(
            (LATBLK, half), lambda i, p, c: (jnp.maximum(p[i * CAP + s], 0), c[0])
        )

    return pl.pallas_call(
        body,
        grid_spec=pltpu.PrefetchScalarGridSpec(
            num_scalar_prefetch=2,
            grid=(blocks,),
            in_specs=[spec(s) for s in range(CAP)],
            out_specs=pl.BlockSpec((None, SLOT, half), lambda i, p, c: (i, 0, 0)),
        ),
        out_shape=jax.ShapeDtypeStruct((blocks, SLOT, half), jnp.bfloat16),
        compiler_params=PARAMS,
        cost_estimate=SMALL,
    )(pick, core, *([in_hbm(w_dec)] * CAP))


def whole(shape):
    return pl.BlockSpec(shape, lambda i, *_: (0,) * len(shape))


def slot_specs(weights, offsets):
    return [
        pl.BlockSpec((None, *w.shape[1:]), lambda i, *_, o=o: (o, 0, 0))
        for o in offsets
        for w in weights
    ]


def slots(weights, offsets):
    return [w for _ in offsets for w in weights]


def across(a, b):
    return lax.dot_general(a, b, (((1,), (1,)), ((), ())), preferred_element_type=jnp.float32)


def encode(blocks, weights, offsets, core):
    count = len(blocks)
    rows, half = blocks[0].shape

    def body(core_ref, *refs):
        out_ref = refs[-1]
        first = core_ref[0] == 0
        for at in range(count):
            own, other = [
                jnp.dot(
                    refs[at][...], refs[count + 2 * at + i][...],
                    preferred_element_type=jnp.float32,
                ).astype(jnp.bfloat16)
                for i in range(2)
            ]
            out_ref[at, :, :SLOT] = jnp.where(first, own, other)
            out_ref[at, :, SLOT:] = jnp.where(first, other, own)

    return pl.pallas_call(
        body,
        grid_spec=pltpu.PrefetchScalarGridSpec(
            num_scalar_prefetch=1,
            grid=(1,),
            in_specs=[whole((rows, half))] * count + slot_specs(weights, offsets),
            out_specs=whole((count, rows, 2 * SLOT)),
        ),
        out_shape=jax.ShapeDtypeStruct((count, rows, 2 * SLOT), jnp.bfloat16),
        compiler_params=PARAMS,
        cost_estimate=SMALL,
    )(core, *[in_vmem(block) for block in blocks], *slots(weights, offsets))


def own_and_other(value, core_ref):
    low, high = value[:, :SLOT], value[:, SLOT:]
    first = core_ref[0] == 0
    return jnp.where(first, low, high), jnp.where(first, high, low)


def decode(pre, biases, weights, offsets, splits, core):
    count, rows, _ = pre.shape
    half = weights[0].shape[2]

    def body(core_ref, *refs):
        pre_ref, bias_refs, weight_refs = refs[0], refs[1:3], refs[3 : 3 + 2 * count]
        code_ref, part_refs = refs[3 + 2 * count], refs[4 + 2 * count :]
        for at, offset in enumerate(offsets):
            total = None
            for i, one in enumerate(own_and_other(pre_ref[at], core_ref)):
                code = jnp.maximum(one + bias_refs[i][offset : offset + 1, :], 0.0)
                code = code.astype(jnp.bfloat16)
                code_ref[at, :, i * SLOT : (i + 1) * SLOT] = code
                term = jnp.dot(
                    code, weight_refs[2 * at + i][...], preferred_element_type=jnp.float32
                )
                total = term if total is None else total + term
            step = rows // splits[at]
            for r in range(splits[at]):
                part_ref = part_refs[sum(splits[:at]) + r]
                part_ref[...] = total[r * step : (r + 1) * step].astype(part_ref.dtype)

    shapes = [
        jax.ShapeDtypeStruct((rows // split, half), jnp.bfloat16 if offset % 2 else jnp.float32)
        for offset, split in zip(offsets, splits)
        for _ in range(split)
    ]
    code, *parts = pl.pallas_call(
        body,
        grid_spec=pltpu.PrefetchScalarGridSpec(
            num_scalar_prefetch=1,
            grid=(1,),
            in_specs=[whole(pre.shape)]
            + [whole(bias.shape) for bias in biases]
            + slot_specs(weights, offsets),
            out_specs=[whole(pre.shape)] + [whole(shape.shape) for shape in shapes],
        ),
        out_shape=[jax.ShapeDtypeStruct(pre.shape, jnp.bfloat16)] + shapes,
        compiler_params=PARAMS,
        cost_estimate=SMALL,
    )(core, pre, *biases, *slots(weights, offsets))
    by_offset = {}
    for offset, split in zip(offsets, splits):
        by_offset[offset], parts = parts[:split], parts[split:]
    return code, by_offset


def added(part, arrived):
    def body(part_ref, arrived_ref, out_ref):
        total = part_ref[...].astype(jnp.float32) + arrived_ref[...].astype(jnp.float32)
        out_ref[...] = total.astype(jnp.bfloat16)

    return pl.pallas_call(
        body,
        grid=(1,),
        in_specs=[whole(part.shape)] * 2,
        out_specs=whole(part.shape),
        out_shape=jax.ShapeDtypeStruct(part.shape, jnp.bfloat16),
        compiler_params=PARAMS,
        cost_estimate=SMALL,
    )(part, arrived)


def remainder(part, arrived, bias, tokens, core, r, rows):
    half = part.shape[1]

    def body(core_ref, part_ref, bias_ref, token_ref, *refs):
        total = part_ref[...]
        for arrived_ref in refs[:-1]:
            total = total + arrived_ref[...].astype(jnp.float32)
        total = total + bias_ref[...]
        refs[-1][...] = (total - token_ref[...].astype(jnp.float32)).astype(jnp.bfloat16)

    def at_part(value):
        return pl.BlockSpec((rows, half), lambda i, c: (r if value.shape[0] > rows else 0, 0))

    return pl.pallas_call(
        body,
        grid_spec=pltpu.PrefetchScalarGridSpec(
            num_scalar_prefetch=1,
            grid=(1,),
            in_specs=[
                at_part(part),
                pl.BlockSpec((1, half), lambda i, c: (0, c[0])),
                at_part(tokens),
            ]
            + [at_part(value) for value in arrived],
            out_specs=pl.BlockSpec((rows, half), lambda i, c: (0, 0)),
        ),
        out_shape=jax.ShapeDtypeStruct((rows, half), jnp.bfloat16),
        compiler_params=PARAMS,
        cost_estimate=SMALL,
    )(core, part, bias, tokens, *arrived)


def gradient(error, codes, at, first, weights, offset, cost=SMALL):
    rows, half = error.shape

    def body(error_ref, code_ref, own_ref, other_ref, out_ref):
        for i, weight_ref in enumerate((own_ref, other_ref)):
            code = code_ref[:, i * SLOT : (i + 1) * SLOT].astype(jnp.float32)
            grad = across(error_ref[...], weight_ref[...])
            out_ref[i : i + 1, :] = jnp.sum(code * grad, axis=0, keepdims=True)

    return pl.pallas_call(
        body,
        grid=(1,),
        in_specs=[
            whole((rows, half)),
            pl.BlockSpec((None, rows, 2 * SLOT), lambda i: (at, first, 0)),
        ]
        + slot_specs(weights, [offset]),
        out_specs=whole((2, SLOT)),
        out_shape=jax.ShapeDtypeStruct((2, SLOT), jnp.float32),
        compiler_params=PARAMS,
        cost_estimate=cost,
    )(error, codes, *slots(weights, [offset]))


def gathered(terms):
    blocks = len(terms)
    flat = [term for block in terms for term in block]
    ends = [sum(len(block) for block in terms[: i + 1]) for i in range(blocks)]

    def body(*refs):
        for o in range(blocks):
            total = None
            for ref in refs[ends[o] - len(terms[o]) : ends[o]]:
                total = ref[...] if total is None else total + ref[...]
            for i in range(2):
                refs[len(flat) + i][o : o + 1, :] = total[i : i + 1, :]

    shape = jax.ShapeDtypeStruct((blocks, SLOT), jnp.float32)
    return pl.pallas_call(
        body,
        grid=(1,),
        in_specs=[whole((2, SLOT))] * len(flat),
        out_specs=[whole(shape.shape)] * 2,
        out_shape=[shape, shape],
        compiler_params=PARAMS,
        cost_estimate=SMALL,
    )(*flat)


def by_latent(total, pick, latents):
    wide = 2 * LATBLK
    blocks = total.shape[0]

    def body(pick_ref, total_ref, out_ref):
        out_ref[...] = jnp.zeros(out_ref.shape, jnp.float32)
        lane = lax.broadcasted_iota(jnp.int32, (1, wide), 1)
        for o in range(blocks):
            for s in range(CAP):
                chosen = pick_ref[o * CAP + s]
                at = jnp.maximum(chosen, 0)
                value = total_ref[o : o + 1, s * LATBLK : (s + 1) * LATBLK] * (1.0 / TBLK)
                here = (lane // LATBLK == lax.rem(at, 2)) & (chosen >= 0)
                row = pl.ds(lax.div(at, 2), 1)
                pair = jnp.concatenate([value, value], axis=1)
                out_ref[row, :] = out_ref[row, :] + jnp.where(here, pair, 0.0)

    return pl.pallas_call(
        body,
        grid_spec=pltpu.PrefetchScalarGridSpec(
            num_scalar_prefetch=1,
            grid=(1,),
            in_specs=[whole(total.shape)],
            out_specs=whole((latents // wide, wide)),
        ),
        out_shape=jax.ShapeDtypeStruct((latents // wide, wide), jnp.float32),
        compiler_params=PARAMS,
        cost_estimate=SMALL,
    )(pick, total).reshape(latents)


def side_by_side(own, other, core):
    parts = len(own)
    rows, half = own[0].shape

    def body(core_ref, *refs):
        out_ref = refs[-1]
        first = core_ref[0] == 0
        for r in range(parts):
            here, there = refs[r][...], refs[parts + r][...]
            at = slice(r * rows, (r + 1) * rows)
            out_ref[at, :half] = jnp.where(first, here, there)
            out_ref[at, half:] = jnp.where(first, there, here)

    return pl.pallas_call(
        body,
        grid_spec=pltpu.PrefetchScalarGridSpec(
            num_scalar_prefetch=1,
            grid=(1,),
            in_specs=[whole((rows, half))] * (2 * parts),
            out_specs=whole((parts * rows, 2 * half)),
        ),
        out_shape=jax.ShapeDtypeStruct((parts * rows, 2 * half), own[0].dtype),
        compiler_params=PARAMS,
        cost_estimate=SMALL,
    )(core, *own, *other)


def on_device(tokens, w_enc, b_enc, w_dec, b_dec, block_ids, counts):
    own_rows, layers_here, width = tokens.shape
    assert own_rows == TBLK and layers_here == 1
    latents_here = w_enc.shape[2]
    device_blocks = latents_here // LATBLK
    half = width // 2
    lat_size = lax.axis_size("lat")
    place = lax.axis_index("lat")
    core = lax.axis_index("tok")
    bf16, f32 = jnp.bfloat16, jnp.float32

    odds = list(range(1, lat_size, 2))
    evens = list(range(2, lat_size, 2))
    core_at = jnp.full((1,), core, jnp.int32)
    own_half = half_of(tokens.reshape(own_rows, width), core_at)
    near_tokens = swap(own_half, "lat", 1)

    own_pick, other_pick, bias_own = plan(
        block_ids, counts, jnp.stack([place, core]).astype(jnp.int32), b_enc
    )
    enc_two = [
        encoder_slots(w_enc[0], own_pick, core_at),
        encoder_slots(swap(w_enc, "tok", 1)[0], other_pick, core_at),
    ]
    dec_own = decoder_slots(w_dec[0], own_pick, core_at)
    biases = (bias_own, swap(bias_own, "tok", 1))
    token_blocks = {0: own_half, 1: swap(own_half, "lat", 1)}
    for mask in reversed(masks_of("lat")):
        if mask > 1:
            for offset in [o for o in token_blocks if o % 2 == 0]:
                token_blocks[offset ^ mask] = swap(token_blocks[offset], "lat", mask)
    even_tokens, enc_two, dec_own, biases = lax.optimization_barrier(
        ([token_blocks[o] for o in evens], enc_two, dec_own, biases)
    )
    for offset, value in zip(evens, even_tokens):
        token_blocks[offset] = value
        token_blocks[offset ^ 1] = swap(value, "lat", 1)

    def encoded(offsets):
        return encode([token_blocks[o] for o in offsets], enc_two, offsets, core_at)

    def both_cores(term, other):
        return (term.astype(f32) + other.astype(f32)).astype(bf16)

    def summed(term, other):
        return sum_layers(both_cores(term, other))

    def forward(pre, offsets, splits):
        return decode(pre, biases, dec_two, offsets, splits, core_at)

    first, far = [*evens, 1], odds[1:]
    own_term, first_term = encoded([0]), encoded(first)
    first_other = swap(first_term, "tok", 1)
    w_dec_other, first_other = lax.optimization_barrier((swap(w_dec, "tok", 1), first_other))
    dec_two = [dec_own, decoder_slots(w_dec_other[0], other_pick, core_at)]
    far_tokens, dec_two = lax.optimization_barrier(([token_blocks[o] for o in far], dec_two))
    token_blocks.update(zip(far, far_tokens))
    first_code, first_parts = forward(
        summed(first_term, first_other), first, [ROW_PARTS] * len(evens) + [1]
    )
    far_term = encoded(far)
    far_sum = summed(far_term, swap(far_term, "tok", 1))
    far_code, far_parts = forward(far_sum, far, [ROW_PARTS] * len(far))

    far_sums = [{o - 1: swap(far_parts[o][r], "lat", 1) for o in far} for r in range(ROW_PARTS)]
    own_both = both_cores(own_term, swap(own_term, "tok", 1))
    own_both, near_part, far_sums[0] = lax.optimization_barrier(
        (own_both, first_parts[1][0], far_sums[0])
    )
    near_sum = swap(near_part, "lat", 1)
    own_code, own_parts = forward(sum_layers(own_both), [0], [1])
    codes = {
        o: (code, at)
        for code, offsets in ((first_code, first), (far_code, far), (own_code, [0]))
        for at, o in enumerate(offsets)
    }
    halves = []
    for r in range(ROW_PARTS):
        arrived = [near_sum]
        held = {o: added(first_parts[o][r], far_sums[r][o]) for o in evens}
        for mask in masks_of("lat")[1:]:
            for o in sorted(held):
                if o & mask:
                    value = swap(held.pop(o), "lat", mask)
                    if o == mask:
                        arrived.append(value)
                    else:
                        held[o ^ mask] = added(held[o ^ mask], value)
        halves.append(
            remainder(
                own_parts[0][0], arrived, b_dec, own_half, core_at, r, own_rows // ROW_PARTS
            )
        )

    terms = [[] for _ in range(lat_size)]
    before = None
    for r in range(ROW_PARTS):
        errors = {0: halves[r]}
        for mask in reversed(masks_of("lat")):
            sources = dict(errors)
            if mask == 1:
                errors[1] = swap(sources.pop(0), "lat", 1)
                last = max(sources)
                sources[last], errors[1] = lax.optimization_barrier((sources[last], errors[1]))
            for o, error in sources.items():
                errors[o ^ mask] = swap(error, "lat", mask)
        before = errors[lat_size - 1]
        for o, error in errors.items():
            terms[o].append(gradient(
                error, *codes[o], r, dec_two, o, SMALL if r else AHEAD
            ))
    own_sum, other_sum = gathered(terms)
    total = own_sum + swap(other_sum, "tok", 1)
    for mask in range(1, lax.axis_size("layer")):
        total = total + swap(own_sum, "layer", mask) + swap_both(other_sum, mask)
    scale_grad = by_latent(total, own_pick, latents_here)
    residual = side_by_side(halves, [swap(half, "tok", 1) for half in halves], core_at)
    return residual.reshape(tokens.shape), scale_grad


def solution(mesh):
    in_specs = (
        P(("groups", "lat"), "layer", None),
        P("layer", None, ("lat", "tok")),
        P(("lat", "tok")),
        P("layer", ("lat", "tok"), None),
        P("layer", None),
        P("groups", None),
        P("groups"),
    )
    out_specs = (P(("groups", "lat"), "layer", None), P(("groups", "lat", "tok")))
    return jax.shard_map(
        on_device, mesh=mesh, in_specs=in_specs, out_specs=out_specs, check_vma=False
    )
```

```python
import jax
import jax.numpy as jnp
from jax import lax
from jax.experimental import pallas as pl
from jax.experimental.pallas import tpu as pltpu
from jax.sharding import PartitionSpec as P

LATBLK = 64
TBLK = 128
CAP = 3
SLOT = CAP * LATBLK
ROW_PARTS = 2
PARAMS = pltpu.CompilerParams(vmem_limit_bytes=16 * 1024 * 1024)
SMALL = pl.CostEstimate(flops=0, bytes_accessed=0, transcendentals=0)
AHEAD = pl.CostEstimate(flops=4000000000, bytes_accessed=0, transcendentals=0)


def swap(value, axis, mask):
    size = lax.axis_size(axis)
    return lax.ppermute(value, axis, [(i, i ^ mask) for i in range(size)])


def swap_both(value, mask):
    size = lax.axis_size("layer")
    pairs = [(2 * i + c, 2 * (i ^ mask) + 1 - c) for i in range(size) for c in range(2)]
    return lax.ppermute(value, ("layer", "tok"), pairs)


def masks_of(axis):
    size = lax.axis_size(axis)
    return [1 << i for i in range(size.bit_length() - 1)]


def sum_layers(value):
    for mask in masks_of("layer"):
        total = value.astype(jnp.float32) + swap(value, "layer", mask).astype(jnp.float32)
        value = total.astype(value.dtype)
    return total


def in_hbm(value):
    return pltpu.with_memory_space_constraint(value, pltpu.HBM)


def in_vmem(value):
    return pltpu.with_memory_space_constraint(value, pltpu.VMEM)


def half_of(tokens, core):
    rows, width = tokens.shape
    half = width // 2

    def body(core_ref, token_ref, out_ref):
        out_ref[...] = token_ref[...]

    return pl.pallas_call(
        body,
        grid_spec=pltpu.PrefetchScalarGridSpec(
            num_scalar_prefetch=1,
            grid=(1,),
            in_specs=[pl.BlockSpec((rows, half), lambda i, c: (0, c[0]))],
            out_specs=pl.BlockSpec((rows, half), lambda i, c: (0, 0)),
        ),
        out_shape=jax.ShapeDtypeStruct((rows, half), tokens.dtype),
        compiler_params=PARAMS,
        cost_estimate=SMALL,
    )(core, in_hbm(tokens))


def plan(block_ids, counts, places, bias):
    block_total, slot_total = block_ids.shape
    latents = bias.shape[0]
    device_blocks = latents // LATBLK
    wide = 2 * LATBLK
    shift = device_blocks.bit_length() - 1
    assert device_blocks == 1 << shift

    def body(ids_ref, counts_ref, places_ref, bias_ref, own_ref, other_ref, out_ref):
        place, core = places_ref[0], places_ref[1]
        pick_refs = (own_ref, other_ref)
        for offset in range(block_total):
            block = place ^ offset
            for pick_ref in pick_refs:
                for s in range(CAP):
                    pick_ref[offset * CAP + s] = -1

            def step(slot, found):
                chosen = ids_ref[block, slot]
                shard = lax.shift_right_logical(chosen, shift)
                local = chosen & (device_blocks - 1)
                live = slot < counts_ref[block]
                new = []
                for i, pick_ref in enumerate(pick_refs):
                    mine = live & (shard == place * 2 + (core ^ i))
                    at = offset * CAP + jnp.minimum(found[i], CAP - 1)

                    @pl.when(mine)
                    def _():
                        pick_ref[at] = local

                    new.append(found[i] + mine.astype(jnp.int32))
                return tuple(new)

            lax.fori_loop(0, slot_total, step, (jnp.int32(0), jnp.int32(0)), unroll=8)
        for offset in range(block_total):
            for s in range(CAP):
                chosen = own_ref[offset * CAP + s]
                at = jnp.maximum(chosen, 0)
                pair = bias_ref[pl.ds(lax.div(at, 2), 1), :]
                row = jnp.where(lax.rem(at, 2) == 1, pair[:, LATBLK:], pair[:, :LATBLK])
                out_ref[offset : offset + 1, s * LATBLK : (s + 1) * LATBLK] = jnp.where(
                    chosen < 0, -jnp.inf, row
                )

    smem = pl.BlockSpec(memory_space=pltpu.SMEM)
    picks = jax.ShapeDtypeStruct((block_total * CAP,), jnp.int32)
    return pl.pallas_call(
        body,
        grid=(1,),
        in_specs=[smem] * 3 + [whole((latents // wide, wide))],
        out_specs=[smem, smem, whole((block_total, SLOT))],
        out_shape=[picks, picks, jax.ShapeDtypeStruct((block_total, SLOT), jnp.float32)],
        compiler_params=PARAMS,
        cost_estimate=SMALL,
    )(in_hbm(block_ids), in_hbm(counts), places, in_hbm(bias.reshape(latents // wide, wide)))


def encoder_slots(w_enc, pick, core):
    half = w_enc.shape[0] // 2
    blocks = pick.shape[0] // CAP

    def body(pick_ref, core_ref, *refs):
        step = pl.program_id(0)
        placed = []
        for s in range(CAP):
            odd = lax.rem(jnp.maximum(pick_ref[step * CAP + s], 0), 2)
            wide = refs[s][...]
            turned = jnp.concatenate([wide[:, LATBLK:], wide[:, :LATBLK]], axis=1)
            placed.append(jnp.where(odd == s % 2, wide, turned))
        low = lax.broadcasted_iota(jnp.int32, placed[0].shape, 1) < LATBLK
        for s in range(0, CAP - 1, 2):
            refs[CAP][:, s * LATBLK : (s + 2) * LATBLK] = jnp.where(
                low, placed[s], placed[s + 1]
            )
        if CAP % 2:
            refs[CAP][:, (CAP - 1) * LATBLK :] = placed[-1][:, :LATBLK]

    def spec(s):
        return pl.BlockSpec(
            (half, 2 * LATBLK),
            lambda i, p, c: (c[0], lax.div(jnp.maximum(p[i * CAP + s], 0), 2)),
        )

    return pl.pallas_call(
        body,
        grid_spec=pltpu.PrefetchScalarGridSpec(
            num_scalar_prefetch=2,
            grid=(blocks,),
            in_specs=[spec(s) for s in range(CAP)],
            out_specs=pl.BlockSpec((None, half, SLOT), lambda i, p, c: (i, 0, 0)),
        ),
        out_shape=jax.ShapeDtypeStruct((blocks, half, SLOT), jnp.bfloat16),
        compiler_params=PARAMS,
        cost_estimate=SMALL,
    )(pick, core, *([in_hbm(w_enc)] * CAP))


def decoder_slots(w_dec, pick, core):
    half = w_dec.shape[1] // 2
    blocks = pick.shape[0] // CAP

    def body(pick_ref, core_ref, *refs):
        for s in range(CAP):
            refs[CAP][s * LATBLK : (s + 1) * LATBLK, :] = refs[s][...]

    def spec(s):
        return pl.BlockSpec(
            (LATBLK, half), lambda i, p, c: (jnp.maximum(p[i * CAP + s], 0), c[0])
        )

    return pl.pallas_call(
        body,
        grid_spec=pltpu.PrefetchScalarGridSpec(
            num_scalar_prefetch=2,
            grid=(blocks,),
            in_specs=[spec(s) for s in range(CAP)],
            out_specs=pl.BlockSpec((None, SLOT, half), lambda i, p, c: (i, 0, 0)),
        ),
        out_shape=jax.ShapeDtypeStruct((blocks, SLOT, half), jnp.bfloat16),
        compiler_params=PARAMS,
        cost_estimate=SMALL,
    )(pick, core, *([in_hbm(w_dec)] * CAP))


def whole(shape):
    return pl.BlockSpec(shape, lambda i, *_: (0,) * len(shape))


def slot_specs(weights, offsets):
    return [
        pl.BlockSpec((None, *w.shape[1:]), lambda i, *_, o=o: (o, 0, 0))
        for o in offsets
        for w in weights
    ]


def slots(weights, offsets):
    return [w for _ in offsets for w in weights]


def across(a, b):
    return lax.dot_general(a, b, (((1,), (1,)), ((), ())), preferred_element_type=jnp.float32)


def encode(blocks, weights, offsets, core):
    count = len(blocks)
    rows, half = blocks[0].shape

    def body(core_ref, *refs):
        out_ref = refs[-1]
        first = core_ref[0] == 0
        for at in range(count):
            own, other = [
                jnp.dot(
                    refs[at][...], refs[count + 2 * at + i][...],
                    preferred_element_type=jnp.float32,
                ).astype(jnp.bfloat16)
                for i in range(2)
            ]
            out_ref[at, :, :SLOT] = jnp.where(first, own, other)
            out_ref[at, :, SLOT:] = jnp.where(first, other, own)

    return pl.pallas_call(
        body,
        grid_spec=pltpu.PrefetchScalarGridSpec(
            num_scalar_prefetch=1,
            grid=(1,),
            in_specs=[whole((rows, half))] * count + slot_specs(weights, offsets),
            out_specs=whole((count, rows, 2 * SLOT)),
        ),
        out_shape=jax.ShapeDtypeStruct((count, rows, 2 * SLOT), jnp.bfloat16),
        compiler_params=PARAMS,
        cost_estimate=SMALL,
    )(core, *[in_vmem(block) for block in blocks], *slots(weights, offsets))


def own_and_other(value, core_ref):
    low, high = value[:, :SLOT], value[:, SLOT:]
    first = core_ref[0] == 0
    return jnp.where(first, low, high), jnp.where(first, high, low)


def decode(pre, biases, weights, offsets, splits, core):
    count, rows, _ = pre.shape
    half = weights[0].shape[2]

    def body(core_ref, *refs):
        pre_ref, bias_refs, weight_refs = refs[0], refs[1:3], refs[3 : 3 + 2 * count]
        code_ref, part_refs = refs[3 + 2 * count], refs[4 + 2 * count :]
        for at, offset in enumerate(offsets):
            total = None
            for i, one in enumerate(own_and_other(pre_ref[at], core_ref)):
                code = jnp.maximum(one + bias_refs[i][offset : offset + 1, :], 0.0)
                code = code.astype(jnp.bfloat16)
                code_ref[at, :, i * SLOT : (i + 1) * SLOT] = code
                term = jnp.dot(
                    code, weight_refs[2 * at + i][...], preferred_element_type=jnp.float32
                )
                total = term if total is None else total + term
            step = rows // splits[at]
            for r in range(splits[at]):
                part_ref = part_refs[sum(splits[:at]) + r]
                part_ref[...] = total[r * step : (r + 1) * step].astype(part_ref.dtype)

    shapes = [
        jax.ShapeDtypeStruct((rows // split, half), jnp.bfloat16 if offset % 2 else jnp.float32)
        for offset, split in zip(offsets, splits)
        for _ in range(split)
    ]
    code, *parts = pl.pallas_call(
        body,
        grid_spec=pltpu.PrefetchScalarGridSpec(
            num_scalar_prefetch=1,
            grid=(1,),
            in_specs=[whole(pre.shape)]
            + [whole(bias.shape) for bias in biases]
            + slot_specs(weights, offsets),
            out_specs=[whole(pre.shape)] + [whole(shape.shape) for shape in shapes],
        ),
        out_shape=[jax.ShapeDtypeStruct(pre.shape, jnp.bfloat16)] + shapes,
        compiler_params=PARAMS,
        cost_estimate=SMALL,
    )(core, pre, *biases, *slots(weights, offsets))
    by_offset = {}
    for offset, split in zip(offsets, splits):
        by_offset[offset], parts = parts[:split], parts[split:]
    return code, by_offset


def added(part, arrived):
    def body(part_ref, arrived_ref, out_ref):
        total = part_ref[...].astype(jnp.float32) + arrived_ref[...].astype(jnp.float32)
        out_ref[...] = total.astype(jnp.bfloat16)

    return pl.pallas_call(
        body,
        grid=(1,),
        in_specs=[whole(part.shape)] * 2,
        out_specs=whole(part.shape),
        out_shape=jax.ShapeDtypeStruct(part.shape, jnp.bfloat16),
        compiler_params=PARAMS,
        cost_estimate=SMALL,
    )(part, arrived)


def remainder(part, arrived, bias, tokens, core, r, rows):
    half = part.shape[1]

    def body(core_ref, part_ref, bias_ref, token_ref, *refs):
        total = part_ref[...]
        for arrived_ref in refs[:-1]:
            total = total + arrived_ref[...].astype(jnp.float32)
        total = total + bias_ref[...]
        refs[-1][...] = (total - token_ref[...].astype(jnp.float32)).astype(jnp.bfloat16)

    def at_part(value):
        return pl.BlockSpec((rows, half), lambda i, c: (r if value.shape[0] > rows else 0, 0))

    return pl.pallas_call(
        body,
        grid_spec=pltpu.PrefetchScalarGridSpec(
            num_scalar_prefetch=1,
            grid=(1,),
            in_specs=[
                at_part(part),
                pl.BlockSpec((1, half), lambda i, c: (0, c[0])),
                at_part(tokens),
            ]
            + [at_part(value) for value in arrived],
            out_specs=pl.BlockSpec((rows, half), lambda i, c: (0, 0)),
        ),
        out_shape=jax.ShapeDtypeStruct((rows, half), jnp.bfloat16),
        compiler_params=PARAMS,
        cost_estimate=SMALL,
    )(core, part, bias, tokens, *arrived)


def gradient(error, codes, at, first, weights, offset, cost=SMALL):
    rows, half = error.shape

    def body(error_ref, code_ref, own_ref, other_ref, out_ref):
        for i, weight_ref in enumerate((own_ref, other_ref)):
            moment = lax.dot_general(
                code_ref[:, i * SLOT : (i + 1) * SLOT], error_ref[...], (((0,), (0,)), ((), ())),
                preferred_element_type=jnp.float32,
            )
            out_ref[i, :] = jnp.sum(moment * weight_ref[...].astype(jnp.float32), axis=1)

    return pl.pallas_call(
        body,
        grid=(1,),
        in_specs=[
            whole((rows, half)),
            pl.BlockSpec((None, rows, 2 * SLOT), lambda i: (at, first, 0)),
        ]
        + slot_specs(weights, [offset]),
        out_specs=whole((2, SLOT)),
        out_shape=jax.ShapeDtypeStruct((2, SLOT), jnp.float32),
        compiler_params=PARAMS,
        cost_estimate=cost,
    )(error, codes, *slots(weights, [offset]))


def gathered(terms):
    blocks = len(terms)
    flat = [term for block in terms for term in block]
    ends = [sum(len(block) for block in terms[: i + 1]) for i in range(blocks)]

    def body(*refs):
        for o in range(blocks):
            total = None
            for ref in refs[ends[o] - len(terms[o]) : ends[o]]:
                total = ref[...] if total is None else total + ref[...]
            for i in range(2):
                refs[len(flat) + i][o : o + 1, :] = total[i : i + 1, :]

    shape = jax.ShapeDtypeStruct((blocks, SLOT), jnp.float32)
    return pl.pallas_call(
        body,
        grid=(1,),
        in_specs=[whole((2, SLOT))] * len(flat),
        out_specs=[whole(shape.shape)] * 2,
        out_shape=[shape, shape],
        compiler_params=PARAMS,
        cost_estimate=SMALL,
    )(*flat)


def by_latent(total, pick, latents):
    wide = 2 * LATBLK
    blocks = total.shape[0]

    def body(pick_ref, total_ref, out_ref):
        out_ref[...] = jnp.zeros(out_ref.shape, jnp.float32)
        lane = lax.broadcasted_iota(jnp.int32, (1, wide), 1)
        for o in range(blocks):
            for s in range(CAP):
                chosen = pick_ref[o * CAP + s]
                at = jnp.maximum(chosen, 0)
                value = total_ref[o : o + 1, s * LATBLK : (s + 1) * LATBLK] * (1.0 / TBLK)
                here = (lane // LATBLK == lax.rem(at, 2)) & (chosen >= 0)
                row = pl.ds(lax.div(at, 2), 1)
                pair = jnp.concatenate([value, value], axis=1)
                out_ref[row, :] = out_ref[row, :] + jnp.where(here, pair, 0.0)

    return pl.pallas_call(
        body,
        grid_spec=pltpu.PrefetchScalarGridSpec(
            num_scalar_prefetch=1,
            grid=(1,),
            in_specs=[whole(total.shape)],
            out_specs=whole((latents // wide, wide)),
        ),
        out_shape=jax.ShapeDtypeStruct((latents // wide, wide), jnp.float32),
        compiler_params=PARAMS,
        cost_estimate=SMALL,
    )(pick, total).reshape(latents)


def side_by_side(own, other, core):
    parts = len(own)
    rows, half = own[0].shape

    def body(core_ref, *refs):
        out_ref = refs[-1]
        first = core_ref[0] == 0
        for r in range(parts):
            here, there = refs[r][...], refs[parts + r][...]
            at = slice(r * rows, (r + 1) * rows)
            out_ref[at, :half] = jnp.where(first, here, there)
            out_ref[at, half:] = jnp.where(first, there, here)

    return pl.pallas_call(
        body,
        grid_spec=pltpu.PrefetchScalarGridSpec(
            num_scalar_prefetch=1,
            grid=(1,),
            in_specs=[whole((rows, half))] * (2 * parts),
            out_specs=whole((parts * rows, 2 * half)),
        ),
        out_shape=jax.ShapeDtypeStruct((parts * rows, 2 * half), own[0].dtype),
        compiler_params=PARAMS,
        cost_estimate=SMALL,
    )(core, *own, *other)


def on_device(tokens, w_enc, b_enc, w_dec, b_dec, block_ids, counts):
    own_rows, layers_here, width = tokens.shape
    assert own_rows == TBLK and layers_here == 1
    latents_here = w_enc.shape[2]
    device_blocks = latents_here // LATBLK
    half = width // 2
    lat_size = lax.axis_size("lat")
    place = lax.axis_index("lat")
    core = lax.axis_index("tok")
    bf16, f32 = jnp.bfloat16, jnp.float32

    odds = list(range(1, lat_size, 2))
    evens = list(range(2, lat_size, 2))
    core_at = jnp.full((1,), core, jnp.int32)
    own_half = half_of(tokens.reshape(own_rows, width), core_at)
    near_tokens = swap(own_half, "lat", 1)

    own_pick, other_pick, bias_own = plan(
        block_ids, counts, jnp.stack([place, core]).astype(jnp.int32), b_enc
    )
    enc_two = [
        encoder_slots(w_enc[0], own_pick, core_at),
        encoder_slots(swap(w_enc, "tok", 1)[0], other_pick, core_at),
    ]
    dec_own = decoder_slots(w_dec[0], own_pick, core_at)
    biases = (bias_own, swap(bias_own, "tok", 1))
    token_blocks = {0: own_half, 1: swap(own_half, "lat", 1)}
    for mask in reversed(masks_of("lat")):
        if mask > 1:
            for offset in [o for o in token_blocks if o % 2 == 0]:
                token_blocks[offset ^ mask] = swap(token_blocks[offset], "lat", mask)
    even_tokens, enc_two, dec_own, biases = lax.optimization_barrier(
        ([token_blocks[o] for o in evens], enc_two, dec_own, biases)
    )
    for offset, value in zip(evens, even_tokens):
        token_blocks[offset] = value
        token_blocks[offset ^ 1] = swap(value, "lat", 1)

    def encoded(offsets):
        return encode([token_blocks[o] for o in offsets], enc_two, offsets, core_at)

    def both_cores(term, other):
        return (term.astype(f32) + other.astype(f32)).astype(bf16)

    def summed(term, other):
        return sum_layers(both_cores(term, other))

    def forward(pre, offsets, splits):
        return decode(pre, biases, dec_two, offsets, splits, core_at)

    first, far = [*evens, 1], odds[1:]
    own_term, first_term = encoded([0]), encoded(first)
    first_other = swap(first_term, "tok", 1)
    w_dec_other, first_other = lax.optimization_barrier((swap(w_dec, "tok", 1), first_other))
    dec_two = [dec_own, decoder_slots(w_dec_other[0], other_pick, core_at)]
    far_tokens, dec_two = lax.optimization_barrier(([token_blocks[o] for o in far], dec_two))
    token_blocks.update(zip(far, far_tokens))
    first_code, first_parts = forward(
        summed(first_term, first_other), first, [ROW_PARTS] * len(evens) + [1]
    )
    far_term = encoded(far)
    far_sum = summed(far_term, swap(far_term, "tok", 1))
    far_code, far_parts = forward(far_sum, far, [ROW_PARTS] * len(far))

    far_sums = [{o - 1: swap(far_parts[o][r], "lat", 1) for o in far} for r in range(ROW_PARTS)]
    own_both = both_cores(own_term, swap(own_term, "tok", 1))
    own_both, near_part, far_sums[0] = lax.optimization_barrier(
        (own_both, first_parts[1][0], far_sums[0])
    )
    near_sum = swap(near_part, "lat", 1)
    own_code, own_parts = forward(sum_layers(own_both), [0], [1])
    codes = {
        o: (code, at)
        for code, offsets in ((first_code, first), (far_code, far), (own_code, [0]))
        for at, o in enumerate(offsets)
    }
    halves = []
    for r in range(ROW_PARTS):
        arrived = [near_sum]
        held = {o: added(first_parts[o][r], far_sums[r][o]) for o in evens}
        for mask in masks_of("lat")[1:]:
            for o in sorted(held):
                if o & mask:
                    value = swap(held.pop(o), "lat", mask)
                    if o == mask:
                        arrived.append(value)
                    else:
                        held[o ^ mask] = added(held[o ^ mask], value)
        halves.append(
            remainder(
                own_parts[0][0], arrived, b_dec, own_half, core_at, r, own_rows // ROW_PARTS
            )
        )

    terms = [[] for _ in range(lat_size)]
    before = None
    for r in range(ROW_PARTS):
        errors = {0: halves[r]}
        for mask in reversed(masks_of("lat")):
            sources = dict(errors)
            if mask == 1:
                errors[1] = swap(sources.pop(0), "lat", 1)
                last = max(sources)
                sources[last], errors[1] = lax.optimization_barrier((sources[last], errors[1]))
            for o, error in sources.items():
                errors[o ^ mask] = swap(error, "lat", mask)
        before = errors[lat_size - 1]
        for o, error in errors.items():
            terms[o].append(gradient(
                error, *codes[o], r, dec_two, o, SMALL if r else AHEAD
            ))
    own_sum, other_sum = gathered(terms)
    total = own_sum + swap(other_sum, "tok", 1)
    for mask in range(1, lax.axis_size("layer")):
        total = total + swap(own_sum, "layer", mask) + swap_both(other_sum, mask)
    scale_grad = by_latent(total, own_pick, latents_here)
    residual = side_by_side(halves, [swap(half, "tok", 1) for half in halves], core_at)
    return residual.reshape(tokens.shape), scale_grad


def solution(mesh):
    in_specs = (
        P(("groups", "lat"), "layer", None),
        P("layer", None, ("lat", "tok")),
        P(("lat", "tok")),
        P("layer", ("lat", "tok"), None),
        P("layer", None),
        P("groups", None),
        P("groups"),
    )
    out_specs = (P(("groups", "lat"), "layer", None), P(("groups", "lat", "tok")))
    return jax.shard_map(
        on_device, mesh=mesh, in_specs=in_specs, out_specs=out_specs, check_vma=False
    )
```
